256 devices in a mesh: dp: 64 (over z, y, x_hi), mp: 4 (over x_lo, core).
Axes of the slice: x: 4 (x_hi: 2, x_lo: 2; x = x_hi * 2 + x_lo), y: 4, z: 8, core: 2. Of those that a mesh axis runs over, the one named last changes fastest.
Arguments:
- frames: bfloat16 [32768, 1024], P('dp'), may hold values from -6 to 6
- norm_gain: float32 [1024], replicated, may hold values from 0.25 to 1.75
- w_inner: bfloat16 [1024, 2048], P(None, 'mp'), may hold values from -0.1875 to 0.1875
- w_outer: bfloat16 [2048, 1024], P('mp'), may hold values from -0.125 to 0.125
- lengths: int32 [64, 8], P('dp'), may hold values from 1 to 256, 512 in all within a row
- frame_mask: int32 [32768], P('dp'), may hold values 0 or 1
- gradient: float32 [1024, 2048], P('dp', 'mp'), may hold values from -0.8 to 0.8
Outputs:
- solution: float32 [1024, 2048], P('dp', 'mp')
- residual: float32 [1024, 2048], P('dp', 'mp')
The draws below stay inside these ranges and needn't reach their ends.
Inputs may be any that keep to these rules, and one draw needn't show every extreme that they name: Each row holds the lengths of one group's 8 utterances and sums to 512.
All inputs are finite; a program needn't handle non-finite values. No bound on the sum of `frame_mask` on one device may be relied on, other than what follows from the above.
Results may differ from the reference program's by a relative error of at most 0.017.
Values may be sent and summed in bfloat16 or wider, within the bound.
A program may use at most 64 MiB of HBM per device.

```python
import math
import jax
import jax.numpy as jnp
import numpy as np
from jax import lax

D = 1024
FF = 2048
TOK_DEV = 512
UTT_DEV = 8
ITERS = 2
TOKENS = 32768
UTTS = 512
N_DP = 64
N_MP = 4


def plant(array, stream_key, smallest, top_value):
    longest = array.shape.index(max(array.shape))
    spots = []
    for shift in (0, 1):
        where = [jax.random.randint(jax.random.fold_in(stream_key, axis), (), 0, length) for axis, length in enumerate(array.shape)]
        where[longest] = (where[longest] + shift) % array.shape[longest]
        spots.append(tuple(where))
    return array.at[spots[0]].set(smallest).at[spots[1]].set(top_value)


def level_of(key, shape, split, low, largest):
    def one(dim, shards_of):
        steps = jax.random.uniform(jax.random.fold_in(jax.random.fold_in(key, 6), dim), (shards_of,), jnp.float32, low / len(split), largest / len(split))
        return jnp.repeat(jnp.exp(steps), shape[dim] // shards_of).reshape((-1,) + (1,) * (len(shape) - dim - 1))

    factor_of = one(*split[0])
    for cut in split[1:]:
        factor_of = factor_of * one(*cut)
    return factor_of


def profile(amount, total, bound, skew):
    loads = [(1 << 20) // math.isqrt(standing ** skew) + 1 for standing in range(2, amount + 1)]
    surplus, holding = total - bound - (amount - 1), [1] * (amount - 1)
    while surplus > 0:
        movable = [i for i in range(amount - 1) if holding[i] < bound]
        whole, remaining = sum([loads[i] for i in movable]), surplus
        for i in movable:
            more = min(bound - holding[i], max(1, remaining * loads[i] // whole), surplus)
            holding[i] = holding[i] + more
            surplus = surplus - more
    return np.array([bound] + holding)


def uneven(stream_key, number_of, total, bound, skew):
    if number_of == 2:
        one = jax.random.randint(stream_key, (), max(1, total - bound), min(bound, total - 1) + 1)
        return jnp.stack([one, total - one])
    sizes = jnp.asarray(profile(number_of, total, bound, skew), jnp.int32)
    pairs = (number_of - 1) // 2
    donor, taker = sizes[1:1 + 2 * pairs:2], sizes[2:2 + 2 * pairs:2]
    margin = jnp.minimum(donor - 1, bound - taker)
    shifted = jax.random.randint(jax.random.fold_in(stream_key, 1), (pairs,), 0, 1 << 20) % (margin + 1)
    sizes = sizes.at[1:1 + 2 * pairs:2].set(donor - shifted).at[2:2 + 2 * pairs:2].set(taker + shifted)
    return sizes[jax.random.permutation(jax.random.fold_in(stream_key, 2), number_of)]


def gaussian(stream_key, extent, deviation, reach, pieces=(), kind=jnp.bfloat16):
    gain = level_of(stream_key, extent, pieces, -0.22, 0.18) if pieces else 1.0
    entries = jax.random.normal(stream_key, extent, jnp.float32) * deviation * gain
    return jnp.minimum(jnp.maximum(entries, -reach), reach).astype(kind)


def setup_inputs(seed: int = 0) -> dict:
    seeds = jax.random.split(jax.random.key(seed), 8)
    frames = gaussian(seeds[0], (TOKENS, D), 1.0, 6.0, ((0, 64),))
    norm_gain = jnp.clip(1.0 + 0.15 * jax.random.normal(seeds[1], (D,), jnp.float32), 0.25, 1.75)
    w_inner = gaussian(seeds[2], (D, FF), D ** -0.5, 0.1875, ((1, 4),))
    w_outer = gaussian(seeds[3], (FF, D), FF ** -0.5, 0.125, ((0, 4),))
    lengths = jax.vmap(lambda own: uneven(own, UTT_DEV, TOK_DEV, TOK_DEV // 2, 2))(jax.random.split(seeds[4], N_DP)).reshape((N_DP, UTT_DEV)).astype(jnp.int32)
    frame_mask = plant((jax.random.randint(seeds[5], (TOKENS,), 0, 8) < 7).astype(jnp.int32), jax.random.fold_in(seeds[5], 1), 0, 1)
    gradient = gaussian(seeds[6], (D, FF), 0.1, 0.8, ((0, 64), (1, 4)), jnp.float32)
    return {"frames": frames, "norm_gain": norm_gain, "w_inner": w_inner, "w_outer": w_outer, "lengths": lengths, "frame_mask": frame_mask, "gradient": gradient}


damping = 0.03

def frame_weights(lengths, frame_mask):
    lens = lengths.astype(jnp.int32)
    ends = jnp.cumsum(lens, axis=1)
    starts = ends - lens
    pos = jnp.arange(TOK_DEV, dtype=jnp.int32)
    inside = (pos[None, :, None] >= starts[:, None, :]) & (pos[None, :, None] < ends[:, None, :])
    inverse = 1.0 / lens.astype(jnp.float32)
    per_frame = lax.optimization_barrier(jnp.sum(jnp.where(inside, inverse[:, None, :], 0.0), axis=2)).reshape(TOKENS)
    return frame_mask.astype(jnp.float32) * per_frame / UTTS

def reference(frames, norm_gain, w_inner, w_outer, lengths, frame_mask, gradient):
    xf = frames.astype(jnp.float32)
    mean = lax.optimization_barrier(jnp.mean(xf, axis=1, keepdims=True))
    var = lax.optimization_barrier(jnp.mean((xf - mean) ** 2, axis=1, keepdims=True))
    normed = (norm_gain * (xf - mean) / jnp.sqrt(var + 1e-05)).astype(jnp.bfloat16)
    pre = jnp.dot(normed, w_inner, preferred_element_type=jnp.float32)
    sig = jax.nn.sigmoid(pre)
    slope = sig * (1.0 + pre * (1.0 - sig))
    weight = frame_weights(lengths, frame_mask)
    block = FF // N_MP

    def curvature(vector):
        vb = vector.astype(jnp.bfloat16)
        q = jnp.dot(normed, vb, preferred_element_type=jnp.float32)
        hq = (0.5 * slope * q).astype(jnp.bfloat16)
        u = jnp.zeros((TOKENS, D), jnp.float32)
        for index in range(N_MP):
            part = jnp.dot(hq[:, index * block:(index + 1) * block], w_outer[index * block:(index + 1) * block], preferred_element_type=jnp.float32)
            part = lax.optimization_barrier(part.astype(jnp.bfloat16))
            u = u + part.astype(jnp.float32)
        gy = (weight[:, None] * u).astype(jnp.bfloat16)
        gh = jnp.dot(gy, w_outer.T, preferred_element_type=jnp.float32)
        ga = (0.5 * slope * gh).astype(jnp.bfloat16)
        return jnp.dot(normed.T, ga, preferred_element_type=jnp.float32) + damping * vector
    solution = jnp.zeros_like(gradient)
    residual = gradient
    direction = gradient
    norm_now = jnp.sum(residual * residual)
    for step in range(ITERS):
        image = curvature(direction)
        alpha = norm_now / jnp.sum(direction * image)
        solution = solution + alpha * direction
        residual = residual - alpha * image
        norm_next = jnp.sum(residual * residual)
        direction = residual + norm_next / norm_now * direction
        norm_now = norm_next
    return (solution, residual)
```

```python
import jax
import jax.numpy as jnp
from jax import lax
from jax.experimental import pallas as pl
from jax.experimental.pallas import tpu as pltpu
from jax.sharding import PartitionSpec as P

MESH = pl.DeviceIdType.MESH
NZ, NW, NM = 8, 8, 4
ROWS = 16
TOK, D, F, HALF = 512, 1024, 512, 512
CH = 128
NT = TOK // CH
BLK = NW * ROWS
DAMPING = 0.03
BF, F32 = jnp.bfloat16, jnp.float32
NEAR = (1, 7, 2, 6, 3, 5, 4)
FAR = (4, 3, 5, 2, 6, 1, 7, 0)


def dot(a, b):
    return jnp.dot(a, b, preferred_element_type=F32)


def fold(p):
    s = jnp.sum(p, axis=0, keepdims=True)
    return s[:, 0:128] + s[:, 128:256] + s[:, 256:384] + s[:, 384:512]


def kernel(
    frames, gain, w_inner, w_outer, lengths, mask, grad, sol, res,
    x, wi, wo, wot, normed, normed_t, hs, wcol,
    v, vd, own, give, got, half, theirs, gy, gyo, ga, term, fromw, toz, fromz, sc_own, sc_in,
    in_sem, zs_sem, zr_sem, ws_sem, wr_sem, cs_sem, cr_sem, ls_sem, lr_sem, gs_sem, gr_sem,
    ts_sem, tr_sem, us_sem, ur_sem, as_sem, ar_sem,
):
    dp, mp = lax.axis_index("dp"), lax.axis_index("mp")
    z, w = dp // NW, dp % NW
    xl, core = mp // 2, mp % 2
    sibling = (dp, xl * 2 + (1 - core))
    partner = (dp, (1 - xl) * 2 + core)

    def zpeer(k):
        return (lax.rem(z + k, NZ) * NW + w, mp)

    def wpeer(k):
        return (z * NW + lax.rem(w + k, NW), mp)

    def mpeer(k):
        return (dp, lax.rem(mp + k, NM))

    def send(src, dst, ssem, rsem, dev):
        pltpu.make_async_remote_copy(
            src_ref=src, dst_ref=dst, send_sem=ssem, recv_sem=rsem, device_id=dev, device_id_type=MESH
        ).start()

    def landed(ref, rsem, dev):
        pltpu.make_async_remote_copy(
            src_ref=ref, dst_ref=ref, send_sem=rsem, recv_sem=rsem, device_id=dev, device_id_type=MESH
        ).wait_recv()

    def sent(ref, ssem, dev):
        pltpu.make_async_remote_copy(
            src_ref=ref, dst_ref=ref, send_sem=ssem, recv_sem=ssem, device_id=dev, device_id_type=MESH
        ).wait_send()

    loads = [
        pltpu.make_async_copy(frames, x, in_sem.at[0]),
        pltpu.make_async_copy(w_inner, wi, in_sem.at[1]),
        pltpu.make_async_copy(w_outer.at[:, pl.ds(pl.multiple_of(core * HALF, HALF), HALF)], wo.at[0], in_sem.at[2]),
        pltpu.make_async_copy(w_outer.at[:, pl.ds(pl.multiple_of((1 - core) * HALF, HALF), HALF)], wo.at[1], in_sem.at[3]),
    ]
    for c in loads:
        c.start()
    v[0, z, w] = grad[...].astype(BF)

    barrier = pltpu.get_barrier_semaphore()
    for k in range(1, NZ):
        pl.semaphore_signal(barrier, inc=1, device_id=zpeer(k), device_id_type=MESH)
    for k in range(1, NW):
        pl.semaphore_signal(barrier, inc=1, device_id=wpeer(k), device_id_type=MESH)
    for k in range(1, NM):
        pl.semaphore_signal(barrier, inc=1, device_id=mpeer(k), device_id_type=MESH)
    pl.semaphore_wait(barrier, NZ + NW + NM - 3)

    def gather_pass(it, block):
        for k in range(1, NW):
            send(v.at[it, block, w], v.at[it, block, w], ws_sem.at[it], wr_sem.at[it], wpeer(k))

    def gather_start(it):
        for k in NEAR:
            send(v.at[it, z, w], v.at[it, z, w], zs_sem.at[it], zr_sem.at[it, k], zpeer(k))
        gather_pass(it, z)

    def gather_forward(it, k):
        block = lax.rem(z + NZ - k, NZ)
        landed(v.at[it, block, w], zr_sem.at[it, k], zpeer(k))
        gather_pass(it, block)

    def gather_end(it):
        landed(v.at[it, pl.ds(0, NW - 1)], wr_sem.at[it], wpeer(1))

    def scal_send(a, phase, tile):
        sc_own[a, phase] = tile
        peers = (mpeer, wpeer, zpeer)[phase]
        for k in range(1, (NM, NW, NZ)[phase]):
            send(sc_own.at[a, phase], sc_in.at[a, phase, k], as_sem.at[a, phase], ar_sem.at[a, phase], peers(k))

    def scal_take(a, phase):
        n = (NM, NW, NZ)[phase]
        landed(sc_in.at[a, phase, pl.ds(1, n - 1)], ar_sem.at[a, phase], (mpeer, wpeer, zpeer)[phase](1))
        tile = sc_own[a, phase]
        for k in range(1, n):
            tile = tile + sc_in[a, phase, k]
        return tile

    gather_start(0)

    ends, end = [], jnp.int32(0)
    starts = []
    for j in range(8):
        starts.append(end)
        end = end + lengths[0, j]
        ends.append(end)
    for t in range(NT):
        pos = lax.broadcasted_iota(jnp.int32, (CH, 128), 0) + t * CH
        per = jnp.zeros((CH, 128), F32)
        for j in range(8):
            inverse = 1.0 / jnp.full((CH, 128), lengths[0, j], jnp.int32).astype(F32)
            per = per + jnp.where((pos >= starts[j]) & (pos < ends[j]), inverse, 0.0)
        rowi = lax.broadcasted_iota(jnp.int32, (CH, 128), 0)
        coli = lax.broadcasted_iota(jnp.int32, (CH, 128), 1)
        m = jnp.broadcast_to(mask[t : t + 1, :].astype(F32), (CH, 128))
        mcol = jnp.sum(jnp.where(rowi == coli, m, 0.0), axis=1, keepdims=True)
        wcol[pl.ds(t * CH, CH), :] = jnp.broadcast_to(mcol, (CH, 128)) * per / 512.0

    def norm_chunk(t):
        rows = pl.ds(t * CH, CH)
        xf = x[rows, :].astype(F32)
        mean = jnp.mean(xf, axis=1, keepdims=True)
        xc = xf - mean
        var = jnp.mean(xc * xc, axis=1, keepdims=True)
        nf = gain[...] * xc / jnp.sqrt(var + 1e-05)
        normed[rows, :] = nf.astype(BF)
        normed_t[:, rows] = nf.T.astype(BF)

    def slope_chunk(t):
        rows = pl.ds(t * CH, CH)
        pre = dot(normed[rows, :], wi[...])
        sig = jax.nn.sigmoid(pre)
        hs[rows, :] = 0.5 * (sig * (1.0 + pre * (1.0 - sig)))

    loads[0].wait()
    for t in range(NT):
        norm_chunk(t)
    gather_forward(0, 1)
    gather_forward(0, 7)
    loads[1].wait()
    slope_chunk(0)
    gather_forward(0, 2)
    gather_forward(0, 6)
    slope_chunk(1)
    gather_forward(0, 3)
    gather_forward(0, 5)
    slope_chunk(2)
    gather_forward(0, 4)
    slope_chunk(3)
    loads[2].wait()
    loads[3].wait()
    for i in range(2):
        wot[i] = wo[i].astype(F32).T.astype(BF)
    gather_end(0)

    def tangent(it, t, mat):
        rows = pl.ds(t * CH, CH)
        q = dot(normed[rows, :], mat)
        hq = (hs[rows, :] * q).astype(BF)
        give[it, t] = dot(hq, wo[1]).astype(BF)
        send(give.at[it, t], got.at[it, t], cs_sem.at[it], cr_sem.at[it, t], sibling)
        own[t] = dot(hq, wo[0])

    def pair_sum(it, t):
        landed(got.at[it, t], cr_sem.at[it, t], sibling)
        half[it, t] = (own[t] + got[it, t].astype(F32)).astype(BF)
        send(half.at[it, t], theirs.at[it, t], ls_sem.at[it], lr_sem.at[it, t], partner)

    def weigh(it, t):
        landed(theirs.at[it, t], lr_sem.at[it, t], partner)
        u = half[it, t].astype(F32) + theirs[it, t].astype(F32)
        wc = wcol[pl.ds(t * CH, CH), :]
        wu = jnp.concatenate([wc] * 4, axis=1) * u
        gy[it, t] = wu.astype(BF)
        send(gy.at[it, t], gyo.at[it, t], gs_sem.at[it], gr_sem.at[it, t], sibling)
        return fold(wu * u)

    def pull_back(it, t):
        landed(gyo.at[it, t], gr_sem.at[it, t], sibling)
        rows = pl.ds(t * CH, CH)
        gh = dot(gy[it, t], wot[0]) + dot(gyo[it, t], wot[1])
        ga[rows, :] = (hs[rows, :] * gh).astype(BF)

    def curve(it, mat):
        tangent(it, 0, mat)
        for t in range(1, NT):
            tangent(it, t, mat)
            pair_sum(it, t - 1)
        pair_sum(it, NT - 1)
        energy = weigh(it, 0)
        for t in range(1, NT):
            energy = energy + weigh(it, t)
            pull_back(it, t - 1)
        pull_back(it, NT - 1)
        return energy

    def terms(it):
        for off in FAR:
            to = lax.rem(z + off, NZ)
            block = dot(normed_t[pl.ds(pl.multiple_of(to * BLK, BLK), BLK), :], ga[...])
            term[it, to] = block.astype(BF).reshape(NW, ROWS, F)
            for k in range(1, NW):
                send(
                    term.at[it, to, lax.rem(w + k, NW)], fromw.at[it, off, k],
                    ts_sem.at[it], tr_sem.at[it, off], wpeer(k),
                )

    def reduce_block(it, off):
        to = lax.rem(z + off, NZ)
        landed(fromw.at[it, off, pl.ds(1, NW - 1)], tr_sem.at[it, off], wpeer(1))
        total = term[it, to, w].astype(F32)
        for k in range(1, NW):
            total = total + fromw[it, off, k].astype(F32)
        if off:
            toz[it, off] = total.astype(BF)
            send(toz.at[it, off], fromz.at[it, off], us_sem.at[it], ur_sem.at[it], zpeer(off))
        return total

    def reduce_end(it, total):
        landed(fromz.at[it, pl.ds(1, NZ - 1)], ur_sem.at[it], zpeer(1))
        for k in range(1, NZ):
            total = total + fromz[it, k].astype(F32)
        return total

    g = grad[...]
    curve(0, v[0].reshape(D, F))
    terms(0)
    for off in FAR:
        total = reduce_block(0, off)
    y0 = reduce_end(0, total)

    v[1, z, w] = y0.astype(BF)
    gather_start(1)
    pad = jnp.zeros((5, 128), F32)
    scal_send(0, 0, jnp.concatenate([fold(g * g), fold(g * y0), fold(y0 * y0), pad], axis=0))
    gather_forward(1, 1)
    gather_forward(1, 7)
    scal_send(0, 1, scal_take(0, 0))
    gather_forward(1, 2)
    gather_forward(1, 6)
    scal_send(0, 2, scal_take(0, 1))
    gather_forward(1, 3)
    gather_forward(1, 5)
    gather_forward(1, 4)
    sums = jnp.sum(scal_take(0, 2), axis=1, keepdims=True)
    gg, gyy, yy = sums[0:1], sums[1:2], sums[2:3]
    alpha0 = gg / (gyy + DAMPING * gg)
    keep = 1.0 - DAMPING * alpha0
    beta = (keep * keep * gg - 2.0 * keep * alpha0 * gyy + alpha0 * alpha0 * yy) / gg
    r1 = g - alpha0 * (y0 + DAMPING * g)
    d1 = r1 + beta * g
    gather_end(1)
    for i in range(NZ):
        g_all = v[0, i].reshape(BLK, F).astype(F32)
        y_all = v[1, i].reshape(BLK, F).astype(F32)
        vd[pl.ds(i * BLK, BLK), :] = ((keep + beta) * g_all - alpha0 * y_all).astype(BF)

    energy = curve(1, vd[...])
    curvature = 0.5 * energy + DAMPING * fold(d1 * d1)
    scal_send(1, 0, jnp.concatenate([curvature, fold(r1 * r1), jnp.zeros((6, 128), F32)], axis=0))
    terms(1)
    scal_send(1, 1, scal_take(1, 0))
    for off in FAR[:4]:
        reduce_block(1, off)
    scal_send(1, 2, scal_take(1, 1))
    for off in FAR[4:]:
        total = reduce_block(1, off)
    ad1 = reduce_end(1, total)
    sums = jnp.sum(scal_take(1, 2), axis=1, keepdims=True)
    alpha1 = sums[1:2] / sums[0:1]
    sol[...] = alpha0 * g + alpha1 * d1
    res[...] = r1 - alpha1 * (ad1 + DAMPING * d1)

    for it in range(2):
        sent(v.at[it, 0, pl.ds(0, NZ - 1)], zs_sem.at[it], zpeer(1))
        sent(v.at[it, pl.ds(0, NW - 1)], ws_sem.at[it], wpeer(1))
        sent(give.at[it], cs_sem.at[it], sibling)
        sent(half.at[it], ls_sem.at[it], partner)
        sent(gy.at[it], gs_sem.at[it], sibling)
        sent(term.at[it, pl.ds(0, NW - 1)], ts_sem.at[it], wpeer(1))
        sent(toz.at[it, pl.ds(1, NZ - 1)], us_sem.at[it], zpeer(1))
        for phase, n in enumerate((NM, NW, NZ)):
            sent(sc_in.at[it, phase, pl.ds(1, n - 1)], as_sem.at[it, phase], mpeer(1))


def on_device(frames, norm_gain, w_inner, w_outer, lengths, frame_mask, gradient):
    hbm = pl.BlockSpec(memory_space=pl.ANY)
    vmem = pl.BlockSpec(memory_space=pltpu.VMEM)
    smem = pl.BlockSpec(memory_space=pltpu.SMEM)
    dma = pltpu.SemaphoreType.DMA
    out = jax.ShapeDtypeStruct((ROWS, F), F32)
    return tuple(
        pl.pallas_call(
            kernel,
            out_shape=(out, out),
            in_specs=[hbm, vmem, hbm, hbm, smem, vmem, vmem],
            out_specs=(vmem, vmem),
            scratch_shapes=[
                pltpu.VMEM((TOK, D), BF),
                pltpu.VMEM((D, F), BF),
                pltpu.VMEM((2, F, HALF), BF),
                pltpu.VMEM((2, HALF, F), BF),
                pltpu.VMEM((TOK, D), BF),
                pltpu.VMEM((D, TOK), BF),
                pltpu.VMEM((TOK, F), F32),
                pltpu.VMEM((TOK, 128), F32),
                pltpu.VMEM((2, NZ, NW, ROWS, F), BF),
                pltpu.VMEM((D, F), BF),
                pltpu.VMEM((NT, CH, HALF), F32),
                pltpu.VMEM((2, NT, CH, HALF), BF),
                pltpu.VMEM((2, NT, CH, HALF), BF),
                pltpu.VMEM((2, NT, CH, HALF), BF),
                pltpu.VMEM((2, NT, CH, HALF), BF),
                pltpu.VMEM((2, NT, CH, HALF), BF),
                pltpu.VMEM((2, NT, CH, HALF), BF),
                pltpu.VMEM((TOK, F), BF),
                pltpu.VMEM((2, NZ, NW, ROWS, F), BF),
                pltpu.VMEM((2, NZ, NW, ROWS, F), BF),
                pltpu.VMEM((2, NZ, ROWS, F), BF),
                pltpu.VMEM((2, NZ, ROWS, F), BF),
                pltpu.VMEM((2, 3, 8, 128), F32),
                pltpu.VMEM((2, 3, 8, 8, 128), F32),
                dma((4,)),
                dma((2,)), dma((2, NZ)),
                dma((2,)), dma((2,)),
                dma((2,)), dma((2, NT)),
                dma((2,)), dma((2, NT)),
                dma((2,)), dma((2, NT)),
                dma((2,)), dma((2, NZ)),
                dma((2,)), dma((2,)),
                dma((2, 3)), dma((2, 3)),
            ],
            compiler_params=pltpu.CompilerParams(
                collective_id=0, has_side_effects=True, vmem_limit_bytes=48 << 20
            ),
            cost_estimate=pl.CostEstimate(flops=9 * 2 * TOK * D * F, bytes_accessed=4 << 20, transcendentals=TOK * F),
        )(
            frames, norm_gain.reshape(1, D), w_inner, w_outer, lengths, frame_mask.reshape(NT, CH), gradient,
        )
    )


def solution(mesh):
    return jax.shard_map(
        on_device,
        mesh=mesh,
        in_specs=(
            P("dp", None),
            P(),
            P(None, "mp"),
            P("mp", None),
            P("dp", None),
            P("dp"),
            P("dp", "mp"),
        ),
        out_specs=(P("dp", "mp"), P("dp", "mp")),
        check_vma=False,
    )
```

```python
import jax
import jax.numpy as jnp
from jax import lax
from jax.experimental import pallas as pl
from jax.experimental.pallas import tpu as pltpu
from jax.sharding import PartitionSpec as P

MESH = pl.DeviceIdType.MESH
NZ, NW, NM = 8, 8, 4
ROWS = 16
TOK, D, F, HALF = 512, 1024, 512, 512
CH = 128
NT = TOK // CH
BLK = NW * ROWS
DAMPING = 0.03
BF, F32 = jnp.bfloat16, jnp.float32
NEAR = (1, 7, 2, 6, 3, 5, 4)
FAR = (4, 3, 5, 2, 6, 1, 7, 0)


def dot(a, b):
    return jnp.dot(a, b, preferred_element_type=F32)


def fold(p):
    s = jnp.sum(p, axis=0, keepdims=True)
    return s[:, 0:128] + s[:, 128:256] + s[:, 256:384] + s[:, 384:512]


def kernel(
    frames, gain_in, w_inner, w_outer, lengths, mask_in, grad_in, sol, res,
    grad, gain, mask, x, wi, wo, wot, normed, normed_t, hs, wcol,
    v, vd, own, give, got, half, theirs, gy, gyo, ga, term, fromw, toz, fromz, sc_own, sc_in,
    in_sem, zs_sem, zr_sem, ws_sem, wr_sem, cs_sem, cr_sem, ls_sem, lr_sem, gs_sem, gr_sem,
    ts_sem, tr_sem, us_sem, ur_sem, as_sem, ar_sem,
):
    dp, mp = lax.axis_index("dp"), lax.axis_index("mp")
    z, w = dp // NW, dp % NW
    xl, core = mp // 2, mp % 2
    sibling = (dp, xl * 2 + (1 - core))
    partner = (dp, (1 - xl) * 2 + core)

    def zpeer(k):
        return (lax.rem(z + k, NZ) * NW + w, mp)

    def wpeer(k):
        return (z * NW + lax.rem(w + k, NW), mp)

    def mpeer(k):
        return (dp, lax.rem(mp + k, NM))

    def send(src, dst, ssem, rsem, dev):
        pltpu.make_async_remote_copy(
            src_ref=src, dst_ref=dst, send_sem=ssem, recv_sem=rsem, device_id=dev, device_id_type=MESH
        ).start()

    def landed(ref, rsem, dev):
        pltpu.make_async_remote_copy(
            src_ref=ref, dst_ref=ref, send_sem=rsem, recv_sem=rsem, device_id=dev, device_id_type=MESH
        ).wait_recv()

    def sent(ref, ssem, dev):
        pltpu.make_async_remote_copy(
            src_ref=ref, dst_ref=ref, send_sem=ssem, recv_sem=ssem, device_id=dev, device_id_type=MESH
        ).wait_send()

    small = [
        pltpu.make_async_copy(grad_in, grad, in_sem.at[4]),
        pltpu.make_async_copy(gain_in, gain, in_sem.at[5]),
        pltpu.make_async_copy(mask_in, mask, in_sem.at[6]),
    ]
    for c in small:
        c.start()
    loads = [
        pltpu.make_async_copy(frames, x, in_sem.at[0]),
        pltpu.make_async_copy(w_inner, wi, in_sem.at[1]),
        pltpu.make_async_copy(w_outer.at[:, pl.ds(pl.multiple_of(core * HALF, HALF), HALF)], wo.at[0], in_sem.at[2]),
        pltpu.make_async_copy(w_outer.at[:, pl.ds(pl.multiple_of((1 - core) * HALF, HALF), HALF)], wo.at[1], in_sem.at[3]),
    ]
    for c in loads:
        c.start()
    barrier = pltpu.get_barrier_semaphore()
    for k in range(1, NZ):
        pl.semaphore_signal(barrier, inc=1, device_id=zpeer(k), device_id_type=MESH)
    for k in range(1, NW):
        pl.semaphore_signal(barrier, inc=1, device_id=wpeer(k), device_id_type=MESH)
    for k in range(1, NM):
        pl.semaphore_signal(barrier, inc=1, device_id=mpeer(k), device_id_type=MESH)
    for c in small:
        c.wait()
    v[0, z, w] = grad[...].astype(BF)
    pl.semaphore_wait(barrier, NZ + NW + NM - 3)

    def gather_pass(it, block):
        for k in range(1, NW):
            send(v.at[it, block, w], v.at[it, block, w], ws_sem.at[it], wr_sem.at[it], wpeer(k))

    def gather_start(it):
        for k in NEAR:
            send(v.at[it, z, w], v.at[it, z, w], zs_sem.at[it], zr_sem.at[it, k], zpeer(k))
        gather_pass(it, z)

    def gather_forward(it, k):
        block = lax.rem(z + NZ - k, NZ)
        landed(v.at[it, block, w], zr_sem.at[it, k], zpeer(k))
        gather_pass(it, block)

    def gather_end(it):
        landed(v.at[it, pl.ds(0, NW - 1)], wr_sem.at[it], wpeer(1))

    peers_of = (mpeer, wpeer, zpeer, lambda k: sibling)
    count_of = (NM, NW, NZ, 2)

    def scal_send(a, phase, kind, tile):
        sc_own[a, phase] = tile
        for k in range(1, count_of[kind]):
            send(sc_own.at[a, phase], sc_in.at[a, phase, k], as_sem.at[a, phase], ar_sem.at[a, phase], peers_of[kind](k))

    def scal_take(a, phase, kind):
        n = count_of[kind]
        landed(sc_in.at[a, phase, pl.ds(1, n - 1)], ar_sem.at[a, phase], peers_of[kind](1))
        tile = sc_own[a, phase]
        for k in range(1, n):
            tile = tile + sc_in[a, phase, k]
        return tile

    gather_start(0)

    ends, end = [], jnp.int32(0)
    starts = []
    for j in range(8):
        starts.append(end)
        end = end + lengths[0, j]
        ends.append(end)
    for t in range(NT):
        pos = lax.broadcasted_iota(jnp.int32, (CH, 128), 0) + t * CH
        per = jnp.zeros((CH, 128), F32)
        for j in range(8):
            inverse = 1.0 / jnp.full((CH, 128), lengths[0, j], jnp.int32).astype(F32)
            per = per + jnp.where((pos >= starts[j]) & (pos < ends[j]), inverse, 0.0)
        rowi = lax.broadcasted_iota(jnp.int32, (CH, 128), 0)
        coli = lax.broadcasted_iota(jnp.int32, (CH, 128), 1)
        m = jnp.broadcast_to(mask[t : t + 1, :].astype(F32), (CH, 128))
        mcol = jnp.sum(jnp.where(rowi == coli, m, 0.0), axis=1, keepdims=True)
        wcol[pl.ds(t * CH, CH), :] = jnp.broadcast_to(mcol, (CH, 128)) * per / 512.0

    def norm_chunk(t):
        rows = pl.ds(t * CH, CH)
        xf = x[rows, :].astype(F32)
        mean = jnp.mean(xf, axis=1, keepdims=True)
        xc = xf - mean
        var = jnp.mean(xc * xc, axis=1, keepdims=True)
        nf = gain[...] * xc / jnp.sqrt(var + 1e-05)
        normed[rows, :] = nf.astype(BF)
        normed_t[:, rows] = nf.T.astype(BF)

    def slope_chunk(t):
        rows = pl.ds(t * CH, CH)
        pre = dot(normed[rows, :], wi[...])
        sig = jax.nn.sigmoid(pre)
        hs[rows, :] = 0.5 * (sig * (1.0 + pre * (1.0 - sig)))

    loads[0].wait()
    for t in range(NT):
        norm_chunk(t)
    gather_forward(0, 1)
    gather_forward(0, 7)
    loads[1].wait()
    slope_chunk(0)
    gather_forward(0, 2)
    gather_forward(0, 6)
    slope_chunk(1)
    gather_forward(0, 3)
    gather_forward(0, 5)
    slope_chunk(2)
    gather_forward(0, 4)
    slope_chunk(3)
    loads[2].wait()
    loads[3].wait()
    for i in range(2):
        wot[i] = wo[i].astype(F32).T.astype(BF)
    gather_end(0)

    def tangent(it, t, mat):
        rows = pl.ds(t * CH, CH)
        q = dot(normed[rows, :], mat)
        hq = (hs[rows, :] * q).astype(BF)
        give[it, t] = dot(hq, wo[1]).astype(BF)
        send(give.at[it, t], got.at[it, t], cs_sem.at[it], cr_sem.at[it, t], sibling)
        own[t] = dot(hq, wo[0])

    def pair_sum(it, t):
        landed(got.at[it, t], cr_sem.at[it, t], sibling)
        half[it, t] = (own[t] + got[it, t].astype(F32)).astype(BF)
        send(half.at[it, t], theirs.at[it, t], ls_sem.at[it], lr_sem.at[it, t], partner)

    def weigh(it, t):
        landed(theirs.at[it, t], lr_sem.at[it, t], partner)
        u = half[it, t].astype(F32) + theirs[it, t].astype(F32)
        wc = wcol[pl.ds(t * CH, CH), :]
        wu = jnp.concatenate([wc] * 4, axis=1) * u
        gy[it, t] = wu.astype(BF)
        send(gy.at[it, t], gyo.at[it, t], gs_sem.at[it], gr_sem.at[it, t], sibling)
        return fold(wu * u)

    def pull_back(it, t):
        landed(gyo.at[it, t], gr_sem.at[it, t], sibling)
        rows = pl.ds(t * CH, CH)
        gh = dot(gy[it, t], wot[0]) + dot(gyo[it, t], wot[1])
        ga[rows, :] = (hs[rows, :] * gh).astype(BF)

    def curve(it, mat, hook0, hook1, hook2):
        tangent(it, 0, mat)
        for t in range(1, NT):
            tangent(it, t, mat)
            pair_sum(it, t - 1)
        pair_sum(it, NT - 1)
        hook0()
        energy = weigh(it, 0)
        for t in range(1, NT):
            energy = energy + weigh(it, t)
            pull_back(it, t - 1)
            if t == 1:
                hook1()
        hook2(energy)
        pull_back(it, NT - 1)

    def terms(it):
        for off in FAR:
            to = lax.rem(z + off, NZ)
            block = dot(normed_t[pl.ds(pl.multiple_of(to * BLK, BLK), BLK), :], ga[...])
            term[it, to] = block.astype(BF).reshape(NW, ROWS, F)
            for k in range(1, NW):
                send(
                    term.at[it, to, lax.rem(w + k, NW)], fromw.at[it, off, k],
                    ts_sem.at[it], tr_sem.at[it, off], wpeer(k),
                )

    def reduce_block(it, off):
        to = lax.rem(z + off, NZ)
        landed(fromw.at[it, off, pl.ds(1, NW - 1)], tr_sem.at[it, off], wpeer(1))
        total = term[it, to, w].astype(F32)
        for k in range(1, NW):
            total = total + fromw[it, off, k].astype(F32)
        if off:
            toz[it, off] = total.astype(BF)
            send(toz.at[it, off], fromz.at[it, off], us_sem.at[it], ur_sem.at[it], zpeer(off))
        return total

    def reduce_end(it, total):
        landed(fromz.at[it, pl.ds(1, NZ - 1)], ur_sem.at[it], zpeer(1))
        for k in range(1, NZ):
            total = total + fromz[it, k].astype(F32)
        return total

    g = grad[...]
    curve(0, v[0].reshape(D, F), lambda: None, lambda: None, lambda energy: None)
    terms(0)
    for off in FAR:
        total = reduce_block(0, off)
    y0 = reduce_end(0, total)

    v[1, z, w] = y0.astype(BF)
    pad = jnp.zeros((5, 128), F32)
    scal_send(0, 0, 0, jnp.concatenate([fold(g * g), fold(g * y0), fold(y0 * y0), pad], axis=0))
    gather_start(1)
    scal_send(0, 1, 1, scal_take(0, 0, 0))
    gather_forward(1, 1)
    gather_forward(1, 7)
    gather_forward(1, 2)
    gather_forward(1, 6)
    gather_forward(1, 3)
    gather_forward(1, 5)
    gather_forward(1, 4)
    scal_send(0, 2, 2, scal_take(0, 1, 1))
    sums = jnp.sum(scal_take(0, 2, 2), axis=1, keepdims=True)
    gg, gyy, yy = sums[0:1], sums[1:2], sums[2:3]
    alpha0 = gg / (gyy + DAMPING * gg)
    keep = 1.0 - DAMPING * alpha0
    beta = (keep * keep * gg - 2.0 * keep * alpha0 * gyy + alpha0 * alpha0 * yy) / gg
    r1 = g - alpha0 * (y0 + DAMPING * g)
    d1 = r1 + beta * g
    gather_end(1)
    for i in range(NZ):
        g_all = v[0, i].reshape(BLK, F).astype(F32)
        y_all = v[1, i].reshape(BLK, F).astype(F32)
        vd[pl.ds(i * BLK, BLK), :] = ((keep + beta) * g_all - alpha0 * y_all).astype(BF)

    scal_send(1, 0, 0, jnp.concatenate([fold(d1 * d1), fold(r1 * r1), jnp.zeros((6, 128), F32)], axis=0))

    def first_hop():
        scal_send(1, 1, 1, scal_take(1, 0, 0))

    def second_hop():
        scal_send(1, 2, 2, scal_take(1, 1, 1))

    def last_hop(energy):
        scal_send(2, 0, 3, jnp.broadcast_to(energy, (8, 128)))

    curve(1, vd[...], first_hop, second_hop, last_hop)
    scal_send(2, 1, 1, scal_take(2, 0, 3))
    terms(1)
    norms = jnp.sum(scal_take(1, 2, 2), axis=1, keepdims=True)
    scal_send(2, 2, 2, scal_take(2, 1, 1))
    for off in FAR:
        total = reduce_block(1, off)
    ad1 = reduce_end(1, total)
    energy = jnp.sum(scal_take(2, 2, 2)[0:1], axis=1, keepdims=True)
    alpha1 = norms[1:2] / (energy + DAMPING * norms[0:1])
    sol[...] = alpha0 * g + alpha1 * d1
    res[...] = r1 - alpha1 * (ad1 + DAMPING * d1)

    for it in range(2):
        sent(v.at[it, 0, pl.ds(0, NZ - 1)], zs_sem.at[it], zpeer(1))
        sent(v.at[it, pl.ds(0, NW - 1)], ws_sem.at[it], wpeer(1))
        sent(give.at[it], cs_sem.at[it], sibling)
        sent(half.at[it], ls_sem.at[it], partner)
        sent(gy.at[it], gs_sem.at[it], sibling)
        sent(term.at[it, pl.ds(0, NW - 1)], ts_sem.at[it], wpeer(1))
        sent(toz.at[it, pl.ds(1, NZ - 1)], us_sem.at[it], zpeer(1))
    for a in range(3):
        for phase, n in enumerate((2 if a == 2 else NM, NW, NZ)):
            sent(sc_in.at[a, phase, pl.ds(1, n - 1)], as_sem.at[a, phase], mpeer(1))


def on_device(frames, norm_gain, w_inner, w_outer, lengths, frame_mask, gradient):
    hbm = pl.BlockSpec(memory_space=pl.ANY)
    vmem = pl.BlockSpec(memory_space=pltpu.VMEM)
    smem = pl.BlockSpec(memory_space=pltpu.SMEM)
    dma = pltpu.SemaphoreType.DMA
    out = jax.ShapeDtypeStruct((ROWS, F), F32)
    return tuple(
        pl.pallas_call(
            kernel,
            out_shape=(out, out),
            in_specs=[hbm, hbm, hbm, hbm, smem, hbm, hbm],
            out_specs=(vmem, vmem),
            scratch_shapes=[
                pltpu.VMEM((ROWS, F), F32),
                pltpu.VMEM((1, D), F32),
                pltpu.VMEM((NT, CH), jnp.int32),
                pltpu.VMEM((TOK, D), BF),
                pltpu.VMEM((D, F), BF),
                pltpu.VMEM((2, F, HALF), BF),
                pltpu.VMEM((2, HALF, F), BF),
                pltpu.VMEM((TOK, D), BF),
                pltpu.VMEM((D, TOK), BF),
                pltpu.VMEM((TOK, F), F32),
                pltpu.VMEM((TOK, 128), F32),
                pltpu.VMEM((2, NZ, NW, ROWS, F), BF),
                pltpu.VMEM((D, F), BF),
                pltpu.VMEM((NT, CH, HALF), F32),
                pltpu.VMEM((2, NT, CH, HALF), BF),
                pltpu.VMEM((2, NT, CH, HALF), BF),
                pltpu.VMEM((2, NT, CH, HALF), BF),
                pltpu.VMEM((2, NT, CH, HALF), BF),
                pltpu.VMEM((2, NT, CH, HALF), BF),
                pltpu.VMEM((2, NT, CH, HALF), BF),
                pltpu.VMEM((TOK, F), BF),
                pltpu.VMEM((2, NZ, NW, ROWS, F), BF),
                pltpu.VMEM((2, NZ, NW, ROWS, F), BF),
                pltpu.VMEM((2, NZ, ROWS, F), BF),
                pltpu.VMEM((2, NZ, ROWS, F), BF),
                pltpu.VMEM((3, 3, 8, 128), F32),
                pltpu.VMEM((3, 3, 8, 8, 128), F32),
                dma((7,)),
                dma((2,)), dma((2, NZ)),
                dma((2,)), dma((2,)),
                dma((2,)), dma((2, NT)),
                dma((2,)), dma((2, NT)),
                dma((2,)), dma((2, NT)),
                dma((2,)), dma((2, NZ)),
                dma((2,)), dma((2,)),
                dma((3, 3)), dma((3, 3)),
            ],
            compiler_params=pltpu.CompilerParams(
                collective_id=0, has_side_effects=True, vmem_limit_bytes=63 << 20
            ),
            cost_estimate=pl.CostEstimate(flops=9 * 2 * TOK * D * F, bytes_accessed=4 << 20, transcendentals=TOK * F),
        )(
            frames, norm_gain.reshape(1, D), w_inner, w_outer, lengths, frame_mask.reshape(NT, CH), gradient,
        )
    )


def solution(mesh):
    return jax.shard_map(
        on_device,
        mesh=mesh,
        in_specs=(
            P("dp", None),
            P(),
            P(None, "mp"),
            P("mp", None),
            P("dp", None),
            P("dp"),
            P("dp", "mp"),
        ),
        out_specs=(P("dp", "mp"), P("dp", "mp")),
        check_vma=False,
    )
```

```python
import jax
import jax.numpy as jnp
from jax import lax
from jax.experimental import pallas as pl
from jax.experimental.pallas import tpu as pltpu
from jax.sharding import PartitionSpec as P

MESH = pl.DeviceIdType.MESH
NZ, NW, NM = 8, 8, 4
ROWS = 16
TOK, D, F, HALF = 512, 1024, 512, 512
CH = 128
SHARE = CH // 2
NT = TOK // CH
BLK = NW * ROWS
DAMPING = 0.03
BF, F32 = jnp.bfloat16, jnp.float32
NEAR = (1, 7, 2, 6, 3, 5, 4)
FAR = (4, 3, 5, 2, 6, 1, 7, 0)
ORDER = (0, 2, 1, 3)


def dot(a, b):
    return jnp.dot(a, b, preferred_element_type=F32)


def fold(p):
    s = jnp.sum(p, axis=0, keepdims=True)
    return s[:, 0:128] + s[:, 128:256] + s[:, 256:384] + s[:, 384:512]


def kernel(
    frames, gain_in, w_inner, w_outer, lengths, mask_in, grad_in, sol, res,
    grad, gain, mask, x, wi, wo, wot, normed, normed_t, hs, wcol,
    wrow, v, u_first, own, give, got, half, theirs, gy, gyo, ga, term, fromw, toz, fromz, sc_own, sc_in,
    in_sem, zs_sem, zr_sem, ws_sem, wr_sem, cs_sem, cr_sem, ls_sem, lr_sem, gs_sem, gr_sem,
    ts_sem, tr_sem, us_sem, ur_sem, as_sem, ar_sem, xs_sem, xr_sem,
):
    dp, mp = lax.axis_index("dp"), lax.axis_index("mp")
    z, w = dp // NW, dp % NW
    xl, core = mp // 2, mp % 2
    sibling = (dp, xl * 2 + (1 - core))
    xh = w % 2
    beside = (dp, (1 - xl) * 2 + core)
    across = (dp + 1 - 2 * xh, (1 - xl) * 2 + core)
    kept, taken = 2 + xl, 3 - xl
    kept_from = 2 + (xh + xl) % 2

    def zpeer(k):
        return (lax.rem(z + k, NZ) * NW + w, mp)

    def wpeer(k):
        return (z * NW + lax.rem(w + k, NW), mp)

    def mpeer(k):
        return (dp, lax.rem(mp + k, NM))

    def send(src, dst, ssem, rsem, dev):
        pltpu.make_async_remote_copy(
            src_ref=src, dst_ref=dst, send_sem=ssem, recv_sem=rsem, device_id=dev, device_id_type=MESH
        ).start()

    def landed(ref, rsem, dev):
        pltpu.make_async_remote_copy(
            src_ref=ref, dst_ref=ref, send_sem=rsem, recv_sem=rsem, device_id=dev, device_id_type=MESH
        ).wait_recv()

    def sent(ref, ssem, dev):
        pltpu.make_async_remote_copy(
            src_ref=ref, dst_ref=ref, send_sem=ssem, recv_sem=ssem, device_id=dev, device_id_type=MESH
        ).wait_send()

    small = [
        pltpu.make_async_copy(grad_in, grad, in_sem.at[4]),
        pltpu.make_async_copy(gain_in, gain, in_sem.at[5]),
        pltpu.make_async_copy(mask_in, mask, in_sem.at[6]),
    ]
    for c in small:
        c.start()
    def chunk(t):
        return pl.ds(pl.multiple_of(t * CH, CH), CH)

    def share(t, c):
        return pl.ds(pl.multiple_of(t * CH + c * SHARE, SHARE), SHARE)

    loads = [
        pltpu.make_async_copy(frames.at[pl.ds(0, 2 * CH)], x.at[pl.ds(0, 2 * CH)], in_sem.at[0]),
        pltpu.make_async_copy(frames.at[chunk(kept_from)], x.at[chunk(kept)], in_sem.at[7]),
        pltpu.make_async_copy(w_inner, wi, in_sem.at[1]),
        pltpu.make_async_copy(w_outer.at[:, pl.ds(pl.multiple_of(core * HALF, HALF), HALF)], wo.at[0], in_sem.at[2]),
        pltpu.make_async_copy(w_outer.at[:, pl.ds(pl.multiple_of((1 - core) * HALF, HALF), HALF)], wo.at[1], in_sem.at[3]),
    ]
    for c in loads:
        c.start()
    barrier = pltpu.get_barrier_semaphore()
    for k in range(1, NZ):
        pl.semaphore_signal(barrier, inc=1, device_id=zpeer(k), device_id_type=MESH)
    for k in range(1, NW):
        pl.semaphore_signal(barrier, inc=1, device_id=wpeer(k), device_id_type=MESH)
    for k in range(1, NM):
        pl.semaphore_signal(barrier, inc=1, device_id=mpeer(k), device_id_type=MESH)
    pl.semaphore_signal(barrier, inc=1, device_id=across, device_id_type=MESH)
    for c in small:
        c.wait()
    v[0, z, w] = grad[...].astype(BF)
    pl.semaphore_wait(barrier, NZ + NW + NM - 2)

    def gather_pass(it, block):
        for k in range(1, NW):
            send(v.at[it, block, w], v.at[it, block, w], ws_sem.at[it], wr_sem.at[it], wpeer(k))

    def gather_start(it):
        for k in NEAR:
            send(v.at[it, z, w], v.at[it, z, w], zs_sem.at[it], zr_sem.at[it, k], zpeer(k))
        gather_pass(it, z)

    def gather_forward(it, k):
        block = lax.rem(z + NZ - k, NZ)
        landed(v.at[it, block, w], zr_sem.at[it, k], zpeer(k))
        gather_pass(it, block)

    def gather_end(it):
        landed(v.at[it, pl.ds(0, NW - 1)], wr_sem.at[it], wpeer(1))

    peers_of = (mpeer, wpeer, zpeer, lambda k: sibling)
    count_of = (NM, NW, NZ, 2)

    def scal_send(a, phase, kind, tile):
        sc_own[a, phase] = tile
        for k in range(1, count_of[kind]):
            send(sc_own.at[a, phase], sc_in.at[a, phase, k], as_sem.at[a, phase], ar_sem.at[a, phase], peers_of[kind](k))

    def scal_take(a, phase, kind):
        n = count_of[kind]
        landed(sc_in.at[a, phase, pl.ds(1, n - 1)], ar_sem.at[a, phase], peers_of[kind](1))
        tile = sc_own[a, phase]
        for k in range(1, n):
            tile = tile + sc_in[a, phase, k]
        return tile

    g = grad[...]
    scal_send(0, 0, 0, jnp.broadcast_to(fold(g * g), (8, 128)))
    gather_start(0)

    send(
        frames.at[share(kept_from, core)], x.at[share(kept, core)], xs_sem.at[0], xr_sem.at[0], across
    )

    ends, end = [], jnp.int32(0)
    starts = []
    for j in range(8):
        starts.append(end)
        end = end + lengths[0, j]
        ends.append(end)

    def weight_row(t):
        pos = lax.broadcasted_iota(jnp.int32, (8, 128), 1) + t * CH
        per = jnp.zeros((8, 128), F32)
        for j in range(8):
            inverse = 1.0 / jnp.full((8, 128), lengths[0, j], jnp.int32).astype(F32)
            per = per + jnp.where((pos >= starts[j]) & (pos < ends[j]), inverse, 0.0)
        return mask[pl.ds(t, 1), :].astype(F32) * per / 512.0

    def weight_column(row):
        rowi = lax.broadcasted_iota(jnp.int32, (CH, 128), 0)
        coli = lax.broadcasted_iota(jnp.int32, (CH, 128), 1)
        spread = jnp.where(rowi == coli, jnp.broadcast_to(row[0:1], (CH, 128)), 0.0)
        return jnp.broadcast_to(jnp.sum(spread, axis=1, keepdims=True), (CH, 128))

    wrow[0] = weight_row(kept_from)
    send(wrow.at[0], wrow.at[1], xs_sem.at[1], xr_sem.at[1], across)
    for t in range(2):
        wcol[chunk(t), :] = weight_column(weight_row(t))
    wcol[chunk(kept), :] = weight_column(wrow[0])

    def norm_chunk(t):
        rows = chunk(t)
        xf = x[rows, :].astype(F32)
        mean = jnp.mean(xf, axis=1, keepdims=True)
        xc = xf - mean
        var = jnp.mean(xc * xc, axis=1, keepdims=True)
        nf = gain[...] * xc / jnp.sqrt(var + 1e-05)
        normed[rows, :] = nf.astype(BF)
        normed_t[:, rows] = nf.T.astype(BF)

    def slope_chunk(t):
        rows = chunk(t)
        pre = dot(normed[rows, :], wi[...])
        sig = jax.nn.sigmoid(pre)
        hs[rows, :] = 0.5 * (sig * (1.0 + pre * (1.0 - sig)))

    loads[0].wait()
    norm_chunk(0)
    norm_chunk(1)
    loads[1].wait()
    norm_chunk(kept)
    scal_send(0, 1, 1, scal_take(0, 0, 0))
    gather_forward(0, 1)
    gather_forward(0, 7)
    landed(x.at[share(taken, core)], xr_sem.at[0], across)
    send(x.at[share(taken, core)], x.at[share(taken, core)], xs_sem.at[2], xr_sem.at[2], sibling)
    loads[2].wait()
    slope_chunk(0)
    gather_forward(0, 2)
    gather_forward(0, 6)
    slope_chunk(1)
    gather_forward(0, 3)
    gather_forward(0, 5)
    gather_forward(0, 4)
    scal_send(0, 2, 2, scal_take(0, 1, 1))
    slope_chunk(kept)
    landed(wrow.at[1], xr_sem.at[1], across)
    wcol[chunk(taken), :] = weight_column(wrow[1])
    loads[3].wait()
    loads[4].wait()
    for i in range(2):
        wot[i] = wo[i].astype(F32).T.astype(BF)
    landed(x.at[share(taken, 1 - core)], xr_sem.at[2], sibling)
    norm_chunk(taken)
    slope_chunk(taken)
    gather_end(0)

    def tangent(it, t, mat):
        rows = chunk(t)
        q = dot(normed[rows, :], mat)
        hq = (hs[rows, :] * q).astype(BF)
        give[it, t] = dot(hq, wo[1]).astype(BF)
        send(give.at[it, t], got.at[it, t], cs_sem.at[it], cr_sem.at[it, t], sibling)
        own[t] = dot(hq, wo[0])

    def pair_sum(it, t):
        landed(got.at[it, t], cr_sem.at[it, t], sibling)
        half[it, t] = (own[t] + got[it, t].astype(F32)).astype(BF)
        send(half.at[it, t], theirs.at[it, t], ls_sem.at[it], lr_sem.at[it, t], across if t > 1 else beside)

    def weigh(it, t, beta):
        landed(theirs.at[it, t], lr_sem.at[it, t], across if t > 1 else beside)
        u = half[it, t].astype(F32) + theirs[it, t].astype(F32)
        if it == 0:
            u_first[t] = u
        else:
            u = u + beta * u_first[t]
        wc = wcol[chunk(t), :]
        wu = jnp.concatenate([wc] * 4, axis=1) * u
        gy[it, t] = wu.astype(BF)
        send(gy.at[it, t], gyo.at[it, t], gs_sem.at[it], gr_sem.at[it, t], sibling)
        return fold(wu * u)

    def pull_back(it, t):
        landed(gyo.at[it, t], gr_sem.at[it, t], sibling)
        rows = chunk(t)
        gh = dot(gy[it, t], wot[0]) + dot(gyo[it, t], wot[1])
        ga[rows, :] = (hs[rows, :] * gh).astype(BF)

    def curve(it, mat, get_beta):
        tangent(it, ORDER[0], mat)
        for i in range(1, NT):
            tangent(it, ORDER[i], mat)
            pair_sum(it, ORDER[i - 1])
        pair_sum(it, ORDER[NT - 1])
        beta = get_beta()
        energy = weigh(it, ORDER[0], beta)
        for i in range(1, NT):
            energy = energy + weigh(it, ORDER[i], beta)
            pull_back(it, ORDER[i - 1])
        scal_send(2 * it + 1, 0, 3, jnp.broadcast_to(energy, (8, 128)))
        pull_back(it, ORDER[NT - 1])
        scal_send(2 * it + 1, 1, 1, scal_take(2 * it + 1, 0, 3))

    def terms(it):
        for off in FAR:
            to = lax.rem(z + off, NZ)
            block = dot(normed_t[pl.ds(pl.multiple_of(to * BLK, BLK), BLK), :], ga[...])
            term[it, to] = block.astype(BF).reshape(NW, ROWS, F)
            for k in range(1, NW):
                send(
                    term.at[it, to, lax.rem(w + k, NW)], fromw.at[it, off, k],
                    ts_sem.at[it], tr_sem.at[it, off], wpeer(k),
                )

    def reduce_block(it, off):
        to = lax.rem(z + off, NZ)
        landed(fromw.at[it, off, pl.ds(1, NW - 1)], tr_sem.at[it, off], wpeer(1))
        total = term[it, to, w].astype(F32)
        for k in range(1, NW):
            total = total + fromw[it, off, k].astype(F32)
        if off:
            toz[it, off] = total.astype(BF)
            send(toz.at[it, off], fromz.at[it, off], us_sem.at[it], ur_sem.at[it], zpeer(off))
        return total

    def reduce_end(it, total):
        landed(fromz.at[it, pl.ds(1, NZ - 1)], ur_sem.at[it], zpeer(1))
        for k in range(1, NZ):
            total = total + fromz[it, k].astype(F32)
        return total

    def reduce(it):
        terms(it)
        scal_send(2 * it + 1, 2, 2, scal_take(2 * it + 1, 1, 1))
        for off in FAR:
            total = reduce_block(it, off)
        total = reduce_end(it, total)
        return total, jnp.sum(scal_take(2 * it + 1, 2, 2)[0:1], axis=1, keepdims=True)

    curve(0, v[0].reshape(D, F), lambda: None)
    gg = jnp.sum(scal_take(0, 2, 2)[0:1], axis=1, keepdims=True)
    ag, energy0 = reduce(0)
    alpha0 = gg / (energy0 + DAMPING * gg)
    r1 = g - alpha0 * (ag + DAMPING * g)
    v[1, z, w] = r1.astype(BF)
    gather_start(1)
    scal_send(2, 0, 0, jnp.concatenate([fold(r1 * r1), fold(r1 * g), jnp.zeros((6, 128), F32)], axis=0))
    gather_forward(1, 1)
    gather_forward(1, 7)
    gather_forward(1, 2)
    gather_forward(1, 6)
    gather_forward(1, 3)
    gather_forward(1, 5)
    gather_forward(1, 4)
    scal_send(2, 1, 1, scal_take(2, 0, 0))
    gather_end(1)
    scal_send(2, 2, 2, scal_take(2, 1, 1))

    norms = []

    def get_beta():
        sums = jnp.sum(scal_take(2, 2, 2), axis=1, keepdims=True)
        norms.extend([sums[0:1], sums[1:2], sums[0:1] / gg])
        return norms[2]

    curve(1, v[1].reshape(D, F), get_beta)
    rr1, rg, beta = norms
    ad1, energy1 = reduce(1)
    d1 = r1 + beta * g
    alpha1 = rr1 / (energy1 + DAMPING * (rr1 + 2.0 * beta * rg + beta * beta * gg))
    sol[...] = alpha0 * g + alpha1 * d1
    res[...] = r1 - alpha1 * (ad1 + DAMPING * d1)

    for it in range(2):
        sent(v.at[it, 0, pl.ds(0, NZ - 1)], zs_sem.at[it], zpeer(1))
        sent(v.at[it, pl.ds(0, NW - 1)], ws_sem.at[it], wpeer(1))
        sent(give.at[it], cs_sem.at[it], sibling)
        sent(half.at[it], ls_sem.at[it], beside)
        sent(gy.at[it], gs_sem.at[it], sibling)
        sent(term.at[it, pl.ds(0, NW - 1)], ts_sem.at[it], wpeer(1))
        sent(toz.at[it, pl.ds(1, NZ - 1)], us_sem.at[it], zpeer(1))
    for a in range(4):
        for phase, n in enumerate((2 if a % 2 else NM, NW, NZ)):
            sent(sc_in.at[a, phase, pl.ds(1, n - 1)], as_sem.at[a, phase], mpeer(1))
    sent(x.at[share(kept, core)], xs_sem.at[0], across)
    sent(wrow.at[0], xs_sem.at[1], across)
    sent(x.at[share(taken, core)], xs_sem.at[2], sibling)


def on_device(frames, norm_gain, w_inner, w_outer, lengths, frame_mask, gradient):
    hbm = pl.BlockSpec(memory_space=pl.ANY)
    vmem = pl.BlockSpec(memory_space=pltpu.VMEM)
    smem = pl.BlockSpec(memory_space=pltpu.SMEM)
    dma = pltpu.SemaphoreType.DMA
    out = jax.ShapeDtypeStruct((ROWS, F), F32)
    return tuple(
        pl.pallas_call(
            kernel,
            out_shape=(out, out),
            in_specs=[hbm, hbm, hbm, hbm, smem, hbm, hbm],
            out_specs=(vmem, vmem),
            scratch_shapes=[
                pltpu.VMEM((ROWS, F), F32),
                pltpu.VMEM((1, D), F32),
                pltpu.VMEM((NT, CH), jnp.int32),
                pltpu.VMEM((TOK, D), BF),
                pltpu.VMEM((D, F), BF),
                pltpu.VMEM((2, F, HALF), BF),
                pltpu.VMEM((2, HALF, F), BF),
                pltpu.VMEM((TOK, D), BF),
                pltpu.VMEM((D, TOK), BF),
                pltpu.VMEM((TOK, F), F32),
                pltpu.VMEM((TOK, 128), F32),
                pltpu.VMEM((2, 8, 128), F32),
                pltpu.VMEM((2, NZ, NW, ROWS, F), BF),
                pltpu.VMEM((NT, CH, HALF), F32),
                pltpu.VMEM((NT, CH, HALF), F32),
                pltpu.VMEM((2, NT, CH, HALF), BF),
                pltpu.VMEM((2, NT, CH, HALF), BF),
                pltpu.VMEM((2, NT, CH, HALF), BF),
                pltpu.VMEM((2, NT, CH, HALF), BF),
                pltpu.VMEM((2, NT, CH, HALF), BF),
                pltpu.VMEM((2, NT, CH, HALF), BF),
                pltpu.VMEM((TOK, F), BF),
                pltpu.VMEM((2, NZ, NW, ROWS, F), BF),
                pltpu.VMEM((2, NZ, NW, ROWS, F), BF),
                pltpu.VMEM((2, NZ, ROWS, F), BF),
                pltpu.VMEM((2, NZ, ROWS, F), BF),
                pltpu.VMEM((4, 3, 8, 128), F32),
                pltpu.VMEM((4, 3, 8, 8, 128), F32),
                dma((8,)),
                dma((2,)), dma((2, NZ)),
                dma((2,)), dma((2,)),
                dma((2,)), dma((2, NT)),
                dma((2,)), dma((2, NT)),
                dma((2,)), dma((2, NT)),
                dma((2,)), dma((2, NZ)),
                dma((2,)), dma((2,)),
                dma((4, 3)), dma((4, 3)),
                dma((3,)), dma((3,)),
            ],
            compiler_params=pltpu.CompilerParams(
                collective_id=0, has_side_effects=True, vmem_limit_bytes=63 << 20
            ),
            cost_estimate=pl.CostEstimate(flops=9 * 2 * TOK * D * F, bytes_accessed=4 << 20, transcendentals=TOK * F),
        )(
            frames, norm_gain.reshape(1, D), w_inner, w_outer, lengths, frame_mask.reshape(NT, CH), gradient,
        )
    )


def solution(mesh):
    return jax.shard_map(
        on_device,
        mesh=mesh,
        in_specs=(
            P("dp", None),
            P(),
            P(None, "mp"),
            P("mp", None),
            P("dp", None),
            P("dp"),
            P("dp", "mp"),
        ),
        out_specs=(P("dp", "mp"), P("dp", "mp")),
        check_vma=False,
    )
```

```python
import jax
import jax.numpy as jnp
from jax import lax
from jax.experimental import pallas as pl
from jax.experimental.pallas import tpu as pltpu
from jax.sharding import PartitionSpec as P

MESH = pl.DeviceIdType.MESH
NZ, NW, NM = 8, 8, 4
ROWS = 16
TOK, D, F, HALF = 512, 1024, 512, 512
CH = 128
SHARE = CH // 2
NT = TOK // CH
BLK = NW * ROWS
CA, CB = 384, 128
DAMPING = 0.03
BF, F32 = jnp.bfloat16, jnp.float32
NEAR = (1, 7, 2, 6, 3, 5, 4)
FAR = (4, 3, 5, 2, 6, 1, 7, 0)
ORDER = (0, 2, 1, 3)


def dot(a, b):
    return jnp.dot(a, b, preferred_element_type=F32)


def fold(p):
    s = jnp.sum(p, axis=0, keepdims=True)
    return s[:, 0:128] + s[:, 128:256] + s[:, 256:384] + s[:, 384:512]


def kernel(
    frames, gain_in, w_inner, w_outer, lengths, mask_in, grad_in, sol, res,
    grad, gain, mask, x, wi, wo, wot, normed, normed_t, hs, wcol,
    wrow, va, vb, u_first, own, give, got, half, theirs, gy, gyo, ga, ta, tb, fromw, toz, fromz, bz, tow, bw, sc_own, sc_in,
    in_sem, zs_sem, zr_sem, ws_sem, wr_sem, cs_sem, cr_sem, ls_sem, lr_sem, gs_sem, gr_sem,
    ts_sem, tr_sem, us_sem, ur_sem, as_sem, ar_sem, xs_sem, xr_sem, bs_sem, br_sem, cbs_sem, cbr_sem,
):
    dp, mp = lax.axis_index("dp"), lax.axis_index("mp")
    z, w = dp // NW, dp % NW
    xl, core = mp // 2, mp % 2
    sibling = (dp, xl * 2 + (1 - core))
    xh = w % 2
    beside = (dp, (1 - xl) * 2 + core)
    across = (dp + 1 - 2 * xh, (1 - xl) * 2 + core)
    kept, taken = 2 + xl, 3 - xl
    kept_from = 2 + (xh + xl) % 2

    def zpeer(k):
        return (lax.rem(z + k, NZ) * NW + w, mp)

    def wpeer(k):
        return (z * NW + lax.rem(w + k, NW), mp)

    def mpeer(k):
        return (dp, lax.rem(mp + k, NM))

    def send(src, dst, ssem, rsem, dev):
        pltpu.make_async_remote_copy(
            src_ref=src, dst_ref=dst, send_sem=ssem, recv_sem=rsem, device_id=dev, device_id_type=MESH
        ).start()

    def landed(ref, rsem, dev):
        pltpu.make_async_remote_copy(
            src_ref=ref, dst_ref=ref, send_sem=rsem, recv_sem=rsem, device_id=dev, device_id_type=MESH
        ).wait_recv()

    def sent(ref, ssem, dev):
        pltpu.make_async_remote_copy(
            src_ref=ref, dst_ref=ref, send_sem=ssem, recv_sem=ssem, device_id=dev, device_id_type=MESH
        ).wait_send()

    small = [
        pltpu.make_async_copy(grad_in, grad, in_sem.at[4]),
        pltpu.make_async_copy(gain_in, gain, in_sem.at[5]),
        pltpu.make_async_copy(mask_in, mask, in_sem.at[6]),
    ]
    for c in small:
        c.start()
    def chunk(t):
        return pl.ds(pl.multiple_of(t * CH, CH), CH)

    def share(t, c):
        return pl.ds(pl.multiple_of(t * CH + c * SHARE, SHARE), SHARE)

    loads = [
        pltpu.make_async_copy(frames.at[pl.ds(0, 2 * CH)], x.at[pl.ds(0, 2 * CH)], in_sem.at[0]),
        pltpu.make_async_copy(frames.at[chunk(kept_from)], x.at[chunk(kept)], in_sem.at[7]),
        pltpu.make_async_copy(w_inner, wi, in_sem.at[1]),
        pltpu.make_async_copy(w_outer.at[:, pl.ds(pl.multiple_of(core * HALF, HALF), HALF)], wo.at[0], in_sem.at[2]),
        pltpu.make_async_copy(w_outer.at[:, pl.ds(pl.multiple_of((1 - core) * HALF, HALF), HALF)], wo.at[1], in_sem.at[3]),
    ]
    for c in loads:
        c.start()
    barrier = pltpu.get_barrier_semaphore()
    for k in range(1, NZ):
        pl.semaphore_signal(barrier, inc=1, device_id=zpeer(k), device_id_type=MESH)
    for k in range(1, NW):
        pl.semaphore_signal(barrier, inc=1, device_id=wpeer(k), device_id_type=MESH)
    for k in range(1, NM):
        pl.semaphore_signal(barrier, inc=1, device_id=mpeer(k), device_id_type=MESH)
    pl.semaphore_signal(barrier, inc=1, device_id=across, device_id_type=MESH)
    for c in small:
        c.wait()
    pl.semaphore_wait(barrier, NZ + NW + NM - 2)

    def gather_pass(it, block):
        for k in range(1, NW):
            send(va.at[it, block, w], va.at[it, block, w], ws_sem.at[it], wr_sem.at[it], wpeer(k))

    def gather_start(it, rows):
        va[it, z, w] = rows[:, :CA]
        vb[it, z, w] = rows[:, CA:]
        for k in NEAR:
            send(va.at[it, z, w], va.at[it, z, w], zs_sem.at[it], zr_sem.at[it, k], zpeer(k))
        for k in range(1, NW):
            send(vb.at[it, z, w], vb.at[it, z, w], bs_sem.at[it, 0], br_sem.at[it, 0], wpeer(k))
        gather_pass(it, z)

    def gather_forward(it, k):
        block = lax.rem(z + NZ - k, NZ)
        landed(va.at[it, block, w], zr_sem.at[it, k], zpeer(k))
        gather_pass(it, block)

    def gather_turn(it):
        landed(vb.at[it, 0, pl.ds(0, NW - 1)], br_sem.at[it, 0], wpeer(1))
        for k in NEAR[::-1]:
            send(vb.at[it, z], vb.at[it, z], bs_sem.at[it, 1], br_sem.at[it, 1], zpeer(k))

    def gather_end(it):
        landed(va.at[it, pl.ds(0, NW - 1)], wr_sem.at[it], wpeer(1))
        landed(vb.at[it, pl.ds(0, NZ - 1)], br_sem.at[it, 1], zpeer(1))

    peers_of = (mpeer, wpeer, zpeer, lambda k: sibling)
    count_of = (NM, NW, NZ, 2)

    def scal_send(a, phase, kind, tile):
        sc_own[a, phase] = tile
        for k in range(1, count_of[kind]):
            send(sc_own.at[a, phase], sc_in.at[a, phase, k], as_sem.at[a, phase], ar_sem.at[a, phase], peers_of[kind](k))

    def scal_take(a, phase, kind):
        n = count_of[kind]
        landed(sc_in.at[a, phase, pl.ds(1, n - 1)], ar_sem.at[a, phase], peers_of[kind](1))
        tile = sc_own[a, phase]
        for k in range(1, n):
            tile = tile + sc_in[a, phase, k]
        return tile

    g = grad[...]
    scal_send(0, 0, 0, jnp.broadcast_to(fold(g * g), (8, 128)))
    gather_start(0, g.astype(BF))

    send(
        frames.at[share(kept_from, core)], x.at[share(kept, core)], xs_sem.at[0], xr_sem.at[0], across
    )

    ends, end = [], jnp.int32(0)
    starts = []
    for j in range(8):
        starts.append(end)
        end = end + lengths[0, j]
        ends.append(end)

    def weight_row(t):
        pos = lax.broadcasted_iota(jnp.int32, (8, 128), 1) + t * CH
        per = jnp.zeros((8, 128), F32)
        for j in range(8):
            inverse = 1.0 / jnp.full((8, 128), lengths[0, j], jnp.int32).astype(F32)
            per = per + jnp.where((pos >= starts[j]) & (pos < ends[j]), inverse, 0.0)
        return mask[pl.ds(t, 1), :].astype(F32) * per / 512.0

    def weight_column(row):
        rowi = lax.broadcasted_iota(jnp.int32, (CH, 128), 0)
        coli = lax.broadcasted_iota(jnp.int32, (CH, 128), 1)
        spread = jnp.where(rowi == coli, jnp.broadcast_to(row[0:1], (CH, 128)), 0.0)
        return jnp.broadcast_to(jnp.sum(spread, axis=1, keepdims=True), (CH, 128))

    wrow[0] = weight_row(kept_from)
    send(wrow.at[0], wrow.at[1], xs_sem.at[1], xr_sem.at[1], across)
    for t in range(2):
        wcol[chunk(t), :] = weight_column(weight_row(t))
    wcol[chunk(kept), :] = weight_column(wrow[0])

    def norm_chunk(t):
        rows = chunk(t)
        xf = x[rows, :].astype(F32)
        mean = jnp.mean(xf, axis=1, keepdims=True)
        xc = xf - mean
        var = jnp.mean(xc * xc, axis=1, keepdims=True)
        nf = gain[...] * xc / jnp.sqrt(var + 1e-05)
        normed[rows, :] = nf.astype(BF)
        normed_t[:, rows] = nf.T.astype(BF)

    def slope_chunk(t):
        rows = chunk(t)
        pre = dot(normed[rows, :], wi[...])
        sig = jax.nn.sigmoid(pre)
        hs[rows, :] = 0.5 * (sig * (1.0 + pre * (1.0 - sig)))

    loads[0].wait()
    norm_chunk(0)
    norm_chunk(1)
    gather_forward(0, 1)
    gather_forward(0, 7)
    gather_turn(0)
    loads[1].wait()
    norm_chunk(kept)
    gather_forward(0, 2)
    gather_forward(0, 6)
    loads[2].wait()
    slope_chunk(0)
    gather_forward(0, 3)
    gather_forward(0, 5)
    gather_forward(0, 4)
    landed(x.at[share(taken, core)], xr_sem.at[0], across)
    send(x.at[share(taken, core)], x.at[share(taken, core)], xs_sem.at[2], xr_sem.at[2], sibling)
    slope_chunk(1)
    slope_chunk(kept)
    loads[3].wait()
    loads[4].wait()
    for i in range(2):
        wot[i] = wo[i].astype(F32).T.astype(BF)
    landed(wrow.at[1], xr_sem.at[1], across)
    wcol[chunk(taken), :] = weight_column(wrow[1])
    landed(x.at[share(taken, 1 - core)], xr_sem.at[2], sibling)
    norm_chunk(taken)
    slope_chunk(taken)
    gather_end(0)

    def tangent(it, t):
        rows = chunk(t)
        mat = jnp.concatenate([va[it].reshape(D, CA), vb[it].reshape(D, CB)], axis=1)
        q = dot(normed[rows, :], mat)
        hq = (hs[rows, :] * q).astype(BF)
        give[it, t] = dot(hq, wo[1]).astype(BF)
        send(give.at[it, t], got.at[it, t], cs_sem.at[it], cr_sem.at[it, t], sibling)
        own[t] = dot(hq, wo[0])

    def pair_sum(it, t):
        landed(got.at[it, t], cr_sem.at[it, t], sibling)
        half[it, t] = (own[t] + got[it, t].astype(F32)).astype(BF)
        send(half.at[it, t], theirs.at[it, t], ls_sem.at[it], lr_sem.at[it, t], across if t > 1 else beside)

    def weigh(it, t, beta):
        landed(theirs.at[it, t], lr_sem.at[it, t], across if t > 1 else beside)
        u = half[it, t].astype(F32) + theirs[it, t].astype(F32)
        if it == 0:
            u_first[t] = u
        else:
            u = u + beta * u_first[t]
        wc = wcol[chunk(t), :]
        wu = jnp.concatenate([wc] * 4, axis=1) * u
        gy[it, t] = wu.astype(BF)
        send(gy.at[it, t], gyo.at[it, t], gs_sem.at[it], gr_sem.at[it, t], sibling)
        return fold(wu * u)

    def pull_back(it, t):
        landed(gyo.at[it, t], gr_sem.at[it, t], sibling)
        rows = chunk(t)
        gh = dot(gy[it, t], wot[0]) + dot(gyo[it, t], wot[1])
        ga[rows, :] = (hs[rows, :] * gh).astype(BF)

    def curve(it, get_beta):
        tangent(it, ORDER[0])
        for i in range(1, NT):
            tangent(it, ORDER[i])
            pair_sum(it, ORDER[i - 1])
        pair_sum(it, ORDER[NT - 1])
        beta = get_beta()
        energy = weigh(it, ORDER[0], beta)
        for i in range(1, NT):
            energy = energy + weigh(it, ORDER[i], beta)
            pull_back(it, ORDER[i - 1])
        scal_send(2 * it + 1, 0, 3, jnp.broadcast_to(energy, (8, 128)))
        pull_back(it, ORDER[NT - 1])

    def terms(it):
        for off in FAR:
            to = lax.rem(z + off, NZ)
            block = dot(normed_t[pl.ds(pl.multiple_of(to * BLK, BLK), BLK), :], ga[...]).astype(BF)
            ta[it, to] = block[:, :CA].reshape(NW, ROWS, CA)
            tb[it, to] = block[:, CA:].reshape(NW, ROWS, CB)
            if off:
                send(tb.at[it, to], bz.at[it, off], cbs_sem.at[it, 0], cbr_sem.at[it, 0], zpeer(off))
            for k in range(1, NW):
                send(
                    ta.at[it, to, lax.rem(w + k, NW)], fromw.at[it, off, k],
                    ts_sem.at[it], tr_sem.at[it, off], wpeer(k),
                )

    def reduce_block(it, off):
        to = lax.rem(z + off, NZ)
        landed(fromw.at[it, off, pl.ds(1, NW - 1)], tr_sem.at[it, off], wpeer(1))
        total = ta[it, to, w].astype(F32)
        for k in range(1, NW):
            total = total + fromw[it, off, k].astype(F32)
        if off:
            toz[it, off] = total.astype(BF)
            send(toz.at[it, off], fromz.at[it, off], us_sem.at[it], ur_sem.at[it], zpeer(off))
        return total

    def reduce_turn(it):
        landed(bz.at[it, pl.ds(1, NZ - 1)], cbr_sem.at[it, 0], zpeer(1))
        total = tb[it, z].astype(F32)
        for k in range(1, NZ):
            total = total + bz[it, k].astype(F32)
        tow[it] = total.astype(BF)
        for k in range(1, NW):
            send(tow.at[it, lax.rem(w + k, NW)], bw.at[it, k], cbs_sem.at[it, 1], cbr_sem.at[it, 1], wpeer(k))

    def reduce_end(it, total):
        landed(bw.at[it, pl.ds(1, NW - 1)], cbr_sem.at[it, 1], wpeer(1))
        total_b = tow[it, w].astype(F32)
        for k in range(1, NW):
            total_b = total_b + bw[it, k].astype(F32)
        landed(fromz.at[it, pl.ds(1, NZ - 1)], ur_sem.at[it], zpeer(1))
        for k in range(1, NZ):
            total = total + fromz[it, k].astype(F32)
        return jnp.concatenate([total, total_b], axis=1)

    def reduce(it, extra):
        pair = scal_take(2 * it + 1, 0, 3)
        if extra is not None:
            pair = jnp.concatenate([pair[0:1], extra[0:1], pair[2:8]], axis=0)
        scal_send(2 * it + 1, 1, 1, pair)
        terms(it)
        scal_send(2 * it + 1, 2, 2, scal_take(2 * it + 1, 1, 1))
        for off in FAR[:5]:
            reduce_block(it, off)
        reduce_turn(it)
        for off in FAR[5:]:
            total = reduce_block(it, off)
        total = reduce_end(it, total)
        return total, jnp.sum(scal_take(2 * it + 1, 2, 2), axis=1, keepdims=True)

    curve(0, lambda: None)
    ag, sums = reduce(0, scal_take(0, 0, 0))
    energy0, gg = sums[0:1], sums[1:2]
    alpha0 = gg / (energy0 + DAMPING * gg)
    r1 = g - alpha0 * (ag + DAMPING * g)
    gather_start(1, r1.astype(BF))
    scal_send(2, 0, 0, jnp.concatenate([fold(r1 * r1), fold(r1 * g), jnp.zeros((6, 128), F32)], axis=0))
    gather_forward(1, 1)
    gather_forward(1, 7)
    scal_send(2, 1, 1, scal_take(2, 0, 0))
    gather_turn(1)
    gather_forward(1, 2)
    gather_forward(1, 6)
    gather_forward(1, 3)
    gather_forward(1, 5)
    gather_forward(1, 4)
    scal_send(2, 2, 2, scal_take(2, 1, 1))
    gather_end(1)
    norms = []

    def get_beta():
        sums = jnp.sum(scal_take(2, 2, 2), axis=1, keepdims=True)
        norms.extend([sums[0:1], sums[1:2], sums[0:1] / gg])
        return norms[2]

    curve(1, get_beta)
    rr1, rg, beta = norms
    ad1, sums = reduce(1, None)
    energy1 = sums[0:1]
    d1 = r1 + beta * g
    alpha1 = rr1 / (energy1 + DAMPING * (rr1 + 2.0 * beta * rg + beta * beta * gg))
    sol[...] = alpha0 * g + alpha1 * d1
    res[...] = r1 - alpha1 * (ad1 + DAMPING * d1)

    for it in range(2):
        sent(va.at[it, 0, pl.ds(0, NZ - 1)], zs_sem.at[it], zpeer(1))
        sent(va.at[it, pl.ds(0, NW - 1)], ws_sem.at[it], wpeer(1))
        sent(vb.at[it, 0, pl.ds(0, NW - 1)], bs_sem.at[it, 0], wpeer(1))
        sent(vb.at[it, pl.ds(0, NZ - 1)], bs_sem.at[it, 1], zpeer(1))
        sent(tb.at[it, pl.ds(0, NZ - 1)], cbs_sem.at[it, 0], zpeer(1))
        sent(tow.at[it, pl.ds(0, NW - 1)], cbs_sem.at[it, 1], wpeer(1))
        sent(give.at[it], cs_sem.at[it], sibling)
        sent(half.at[it], ls_sem.at[it], beside)
        sent(gy.at[it], gs_sem.at[it], sibling)
        sent(ta.at[it, pl.ds(0, NW - 1)], ts_sem.at[it], wpeer(1))
        sent(toz.at[it, pl.ds(1, NZ - 1)], us_sem.at[it], zpeer(1))
    for a in range(4):
        for phase, n in enumerate(((NM,), (2, NW, NZ), (NM, NW, NZ), (2, NW, NZ))[a]):
            sent(sc_in.at[a, phase, pl.ds(1, n - 1)], as_sem.at[a, phase], mpeer(1))
    sent(x.at[share(kept, core)], xs_sem.at[0], across)
    sent(wrow.at[0], xs_sem.at[1], across)
    sent(x.at[share(taken, core)], xs_sem.at[2], sibling)


def on_device(frames, norm_gain, w_inner, w_outer, lengths, frame_mask, gradient):
    hbm = pl.BlockSpec(memory_space=pl.ANY)
    vmem = pl.BlockSpec(memory_space=pltpu.VMEM)
    smem = pl.BlockSpec(memory_space=pltpu.SMEM)
    dma = pltpu.SemaphoreType.DMA
    out = jax.ShapeDtypeStruct((ROWS, F), F32)
    return tuple(
        pl.pallas_call(
            kernel,
            out_shape=(out, out),
            in_specs=[hbm, hbm, hbm, hbm, smem, hbm, hbm],
            out_specs=(vmem, vmem),
            scratch_shapes=[
                pltpu.VMEM((ROWS, F), F32),
                pltpu.VMEM((1, D), F32),
                pltpu.VMEM((NT, CH), jnp.int32),
                pltpu.VMEM((TOK, D), BF),
                pltpu.VMEM((D, F), BF),
                pltpu.VMEM((2, F, HALF), BF),
                pltpu.VMEM((2, HALF, F), BF),
                pltpu.VMEM((TOK, D), BF),
                pltpu.VMEM((D, TOK), BF),
                pltpu.VMEM((TOK, F), F32),
                pltpu.VMEM((TOK, 128), F32),
                pltpu.VMEM((2, 8, 128), F32),
                pltpu.VMEM((2, NZ, NW, ROWS, CA), BF),
                pltpu.VMEM((2, NZ, NW, ROWS, CB), BF),
                pltpu.VMEM((NT, CH, HALF), F32),
                pltpu.VMEM((NT, CH, HALF), F32),
                pltpu.VMEM((2, NT, CH, HALF), BF),
                pltpu.VMEM((2, NT, CH, HALF), BF),
                pltpu.VMEM((2, NT, CH, HALF), BF),
                pltpu.VMEM((2, NT, CH, HALF), BF),
                pltpu.VMEM((2, NT, CH, HALF), BF),
                pltpu.VMEM((2, NT, CH, HALF), BF),
                pltpu.VMEM((TOK, F), BF),
                pltpu.VMEM((2, NZ, NW, ROWS, CA), BF),
                pltpu.VMEM((2, NZ, NW, ROWS, CB), BF),
                pltpu.VMEM((2, NZ, NW, ROWS, CA), BF),
                pltpu.VMEM((2, NZ, ROWS, CA), BF),
                pltpu.VMEM((2, NZ, ROWS, CA), BF),
                pltpu.VMEM((2, NZ, NW, ROWS, CB), BF),
                pltpu.VMEM((2, NW, ROWS, CB), BF),
                pltpu.VMEM((2, NW, ROWS, CB), BF),
                pltpu.VMEM((4, 3, 8, 128), F32),
                pltpu.VMEM((4, 3, 8, 8, 128), F32),
                dma((8,)),
                dma((2,)), dma((2, NZ)),
                dma((2,)), dma((2,)),
                dma((2,)), dma((2, NT)),
                dma((2,)), dma((2, NT)),
                dma((2,)), dma((2, NT)),
                dma((2,)), dma((2, NZ)),
                dma((2,)), dma((2,)),
                dma((4, 3)), dma((4, 3)),
                dma((3,)), dma((3,)),
                dma((2, 2)), dma((2, 2)),
                dma((2, 2)), dma((2, 2)),
            ],
            compiler_params=pltpu.CompilerParams(
                collective_id=0, has_side_effects=True, vmem_limit_bytes=63 << 20
            ),
            cost_estimate=pl.CostEstimate(flops=9 * 2 * TOK * D * F, bytes_accessed=4 << 20, transcendentals=TOK * F),
        )(
            frames, norm_gain.reshape(1, D), w_inner, w_outer, lengths, frame_mask.reshape(NT, CH), gradient,
        )
    )


def solution(mesh):
    return jax.shard_map(
        on_device,
        mesh=mesh,
        in_specs=(
            P("dp", None),
            P(),
            P(None, "mp"),
            P("mp", None),
            P("dp", None),
            P("dp"),
            P("dp", "mp"),
        ),
        out_specs=(P("dp", "mp"), P("dp", "mp")),
        check_vma=False,
    )
```

```python
import jax
import jax.numpy as jnp
from jax import lax
from jax.experimental import pallas as pl
from jax.experimental.pallas import tpu as pltpu
from jax.sharding import PartitionSpec as P

MESH = pl.DeviceIdType.MESH
NZ, NW, NM = 8, 8, 4
ROWS = 16
TOK, D, F, HALF = 512, 1024, 512, 512
CH = 128
SHARE = CH // 2
NT = TOK // CH
BLK = NW * ROWS
CA, CB = 384, 128
DAMPING = 0.03
BF, F32 = jnp.bfloat16, jnp.float32
NEAR = (1, 7, 2, 6, 3, 5, 4)
FAR = (4, 3, 5, 2, 6, 1, 7, 0)
WFAR = (3, 5, 7, 1, 4, 2, 6)
ORDER = (0, 2, 1, 3)


def dot(a, b):
    return jnp.dot(a, b, preferred_element_type=F32)


def fold(p):
    s = jnp.sum(p, axis=0, keepdims=True)
    return s[:, 0:128] + s[:, 128:256] + s[:, 256:384] + s[:, 384:512]


def kernel(
    frames, gain_in, w_inner, w_outer, lengths, mask_in, grad_in, out,
    grad, gain, mask, x, wi, wo, wot, normed, normed_t, hs, wcol,
    wrow, va, vb, u_first, own, give, got, half, theirs, gy, gyo, ga, ta, tb, fromw, toz, fromz, bz, tow, bw, sc_own, sc_in,
    in_sem, zs_sem, zr_sem, ws_sem, wr_sem, cs_sem, cr_sem, ls_sem, lr_sem, gs_sem, gr_sem,
    ts_sem, tr_sem, us_sem, ur_sem, as_sem, ar_sem, xs_sem, xr_sem, bs_sem, br_sem, cbs_sem, cbr_sem,
):
    dp, mp = lax.axis_index("dp"), lax.axis_index("mp")
    z, w = dp // NW, dp % NW
    xl, core = mp // 2, mp % 2
    sibling = (dp, xl * 2 + (1 - core))
    xh = w % 2
    beside = (dp, (1 - xl) * 2 + core)
    across = (dp + 1 - 2 * xh, (1 - xl) * 2 + core)
    kept, taken = 2 + xl, 3 - xl
    kept_from = 2 + (xh + xl) % 2

    def zpeer(k):
        return (lax.rem(z + k, NZ) * NW + w, mp)

    def wpeer(k):
        return (z * NW + lax.rem(w + k, NW), mp)

    def mpeer(k):
        return (dp, lax.rem(mp + k, NM))

    def send(src, dst, ssem, rsem, dev):
        pltpu.make_async_remote_copy(
            src_ref=src, dst_ref=dst, send_sem=ssem, recv_sem=rsem, device_id=dev, device_id_type=MESH
        ).start()

    def landed(ref, rsem, dev):
        pltpu.make_async_remote_copy(
            src_ref=ref, dst_ref=ref, send_sem=rsem, recv_sem=rsem, device_id=dev, device_id_type=MESH
        ).wait_recv()

    def sent(ref, ssem, dev):
        pltpu.make_async_remote_copy(
            src_ref=ref, dst_ref=ref, send_sem=ssem, recv_sem=ssem, device_id=dev, device_id_type=MESH
        ).wait_send()

    small = [
        pltpu.make_async_copy(grad_in, grad, in_sem.at[4]),
        pltpu.make_async_copy(gain_in, gain, in_sem.at[5]),
        pltpu.make_async_copy(mask_in, mask, in_sem.at[6]),
    ]
    for c in small:
        c.start()
    def chunk(t):
        return pl.ds(pl.multiple_of(t * CH, CH), CH)

    def share(t, c):
        return pl.ds(pl.multiple_of(t * CH + c * SHARE, SHARE), SHARE)

    loads = [
        pltpu.make_async_copy(frames.at[pl.ds(0, 2 * CH)], x.at[pl.ds(0, 2 * CH)], in_sem.at[0]),
        pltpu.make_async_copy(frames.at[chunk(kept_from)], x.at[chunk(kept)], in_sem.at[7]),
        pltpu.make_async_copy(w_inner, wi, in_sem.at[1]),
        pltpu.make_async_copy(w_outer.at[:, pl.ds(pl.multiple_of(core * HALF, HALF), HALF)], wo.at[0], in_sem.at[2]),
        pltpu.make_async_copy(w_outer.at[:, pl.ds(pl.multiple_of((1 - core) * HALF, HALF), HALF)], wo.at[1], in_sem.at[3]),
    ]
    for c in loads:
        c.start()
    barrier = pltpu.get_barrier_semaphore()
    for k in range(1, NZ):
        pl.semaphore_signal(barrier, inc=1, device_id=zpeer(k), device_id_type=MESH)
    for k in range(1, NW):
        pl.semaphore_signal(barrier, inc=1, device_id=wpeer(k), device_id_type=MESH)
    for k in range(1, NM):
        pl.semaphore_signal(barrier, inc=1, device_id=mpeer(k), device_id_type=MESH)
    pl.semaphore_signal(barrier, inc=1, device_id=across, device_id_type=MESH)
    for c in small:
        c.wait()
    pl.semaphore_wait(barrier, NZ + NW + NM - 2)

    def gather_pass(it, block):
        for k in WFAR:
            send(va.at[it, block, w], va.at[it, block, w], ws_sem.at[it], wr_sem.at[it], wpeer(k))

    def gather_start(it, rows):
        va[it, z, w] = rows[:, :CA]
        vb[it, z, w] = rows[:, CA:]
        for k in NEAR:
            send(va.at[it, z, w], va.at[it, z, w], zs_sem.at[it], zr_sem.at[it, k], zpeer(k))
        for k in WFAR:
            send(vb.at[it, z, w], vb.at[it, z, w], bs_sem.at[it, 0], br_sem.at[it, 0], wpeer(k))
        gather_pass(it, z)

    def gather_forward(it, k):
        block = lax.rem(z + NZ - k, NZ)
        landed(va.at[it, block, w], zr_sem.at[it, k], zpeer(k))
        gather_pass(it, block)

    def gather_turn(it):
        landed(vb.at[it, 0, pl.ds(0, NW - 1)], br_sem.at[it, 0], wpeer(1))
        for k in NEAR[::-1]:
            send(vb.at[it, z], vb.at[it, z], bs_sem.at[it, 1], br_sem.at[it, 1], zpeer(k))

    def gather_end(it):
        landed(va.at[it, pl.ds(0, NW - 1)], wr_sem.at[it], wpeer(1))
        landed(vb.at[it, pl.ds(0, NZ - 1)], br_sem.at[it, 1], zpeer(1))

    peers_of = (mpeer, wpeer, zpeer, lambda k: sibling)
    count_of = (NM, NW, NZ, 2)

    def scal_send(a, phase, kind, tile):
        sc_own[a, phase] = tile
        for k in range(1, count_of[kind]):
            send(sc_own.at[a, phase], sc_in.at[a, phase, k], as_sem.at[a, phase], ar_sem.at[a, phase], peers_of[kind](k))

    def scal_take(a, phase, kind):
        n = count_of[kind]
        landed(sc_in.at[a, phase, pl.ds(1, n - 1)], ar_sem.at[a, phase], peers_of[kind](1))
        tile = sc_own[a, phase]
        for k in range(1, n):
            tile = tile + sc_in[a, phase, k]
        return tile

    g = grad[...]
    scal_send(0, 0, 0, jnp.broadcast_to(fold(g * g), (8, 128)))
    gather_start(0, g.astype(BF))

    send(
        frames.at[share(kept_from, core)], x.at[share(kept, core)], xs_sem.at[0], xr_sem.at[0], across
    )

    ends, end = [], jnp.int32(0)
    starts = []
    for j in range(8):
        starts.append(end)
        end = end + lengths[0, j]
        ends.append(end)

    def weight_row(t):
        pos = lax.broadcasted_iota(jnp.int32, (8, 128), 1) + t * CH
        per = jnp.zeros((8, 128), F32)
        for j in range(8):
            inverse = 1.0 / jnp.full((8, 128), lengths[0, j], jnp.int32).astype(F32)
            per = per + jnp.where((pos >= starts[j]) & (pos < ends[j]), inverse, 0.0)
        return mask[pl.ds(t, 1), :].astype(F32) * per / 512.0

    def weight_column(row):
        rowi = lax.broadcasted_iota(jnp.int32, (CH, 128), 0)
        coli = lax.broadcasted_iota(jnp.int32, (CH, 128), 1)
        spread = jnp.where(rowi == coli, jnp.broadcast_to(row[0:1], (CH, 128)), 0.0)
        return jnp.broadcast_to(jnp.sum(spread, axis=1, keepdims=True), (CH, 128))

    wrow[0] = weight_row(kept_from)
    send(wrow.at[0], wrow.at[1], xs_sem.at[1], xr_sem.at[1], across)
    for t in range(2):
        wcol[chunk(t), :] = weight_column(weight_row(t))
    wcol[chunk(kept), :] = weight_column(wrow[0])

    def norm_chunk(t):
        rows = chunk(t)
        xf = x[rows, :].astype(F32)
        mean = jnp.mean(xf, axis=1, keepdims=True)
        xc = xf - mean
        var = jnp.mean(xc * xc, axis=1, keepdims=True)
        nf = gain[...] * xc / jnp.sqrt(var + 1e-05)
        normed[rows, :] = nf.astype(BF)
        normed_t[:, rows] = nf.T.astype(BF)

    def slope_chunk(t):
        rows = chunk(t)
        pre = dot(normed[rows, :], wi[...])
        sig = jax.nn.sigmoid(pre)
        hs[rows, :] = 0.5 * (sig * (1.0 + pre * (1.0 - sig)))

    loads[0].wait()
    norm_chunk(0)
    norm_chunk(1)
    gather_forward(0, 1)
    gather_forward(0, 7)
    gather_turn(0)
    loads[1].wait()
    norm_chunk(kept)
    gather_forward(0, 2)
    gather_forward(0, 6)
    loads[2].wait()
    slope_chunk(0)
    gather_forward(0, 3)
    gather_forward(0, 5)
    gather_forward(0, 4)
    landed(x.at[share(taken, core)], xr_sem.at[0], across)
    send(x.at[share(taken, core)], x.at[share(taken, core)], xs_sem.at[2], xr_sem.at[2], sibling)
    slope_chunk(1)
    slope_chunk(kept)
    loads[3].wait()
    loads[4].wait()
    for i in range(2):
        wot[i] = wo[i].astype(F32).T.astype(BF)
    landed(wrow.at[1], xr_sem.at[1], across)
    wcol[chunk(taken), :] = weight_column(wrow[1])
    landed(x.at[share(taken, 1 - core)], xr_sem.at[2], sibling)
    norm_chunk(taken)
    slope_chunk(taken)
    gather_end(0)

    def tangent(it, t):
        rows = chunk(t)
        mat = jnp.concatenate([va[it].reshape(D, CA), vb[it].reshape(D, CB)], axis=1)
        q = dot(normed[rows, :], mat)
        hq = (hs[rows, :] * q).astype(BF)
        give[it, t] = dot(hq, wo[1]).astype(BF)
        send(give.at[it, t], got.at[it, t], cs_sem.at[it], cr_sem.at[it, t], sibling)
        own[t] = dot(hq, wo[0])

    def pair_sum(it, t):
        landed(got.at[it, t], cr_sem.at[it, t], sibling)
        half[it, t] = (own[t] + got[it, t].astype(F32)).astype(BF)
        send(half.at[it, t], theirs.at[it, t], ls_sem.at[it], lr_sem.at[it, t], across if t > 1 else beside)

    def weigh(it, t, beta):
        landed(theirs.at[it, t], lr_sem.at[it, t], across if t > 1 else beside)
        u = half[it, t].astype(F32) + theirs[it, t].astype(F32)
        if it == 0:
            u_first[t] = u
        else:
            u = u + beta * u_first[t]
        wc = wcol[chunk(t), :]
        wu = jnp.concatenate([wc] * 4, axis=1) * u
        gy[it, t] = wu.astype(BF)
        send(gy.at[it, t], gyo.at[it, t], gs_sem.at[it], gr_sem.at[it, t], sibling)
        return fold(wu * u)

    def pull_back(it, t):
        landed(gyo.at[it, t], gr_sem.at[it, t], sibling)
        rows = chunk(t)
        gh = dot(gy[it, t], wot[0]) + dot(gyo[it, t], wot[1])
        ga[rows, :] = (hs[rows, :] * gh).astype(BF)

    def curve(it, get_beta):
        tangent(it, ORDER[0])
        for i in range(1, NT):
            tangent(it, ORDER[i])
            pair_sum(it, ORDER[i - 1])
        pair_sum(it, ORDER[NT - 1])
        beta = get_beta()
        energy = weigh(it, ORDER[0], beta)
        for i in range(1, NT):
            energy = energy + weigh(it, ORDER[i], beta)
            pull_back(it, ORDER[i - 1])
        scal_send(2 * it + 1, 0, 3, jnp.broadcast_to(energy, (8, 128)))
        pull_back(it, ORDER[NT - 1])

    def terms(it):
        for off in FAR:
            to = lax.rem(z + off, NZ)
            block = dot(normed_t[pl.ds(pl.multiple_of(to * BLK, BLK), BLK), :], ga[...]).astype(BF)
            ta[it, to] = block[:, :CA].reshape(NW, ROWS, CA)
            tb[it, to] = block[:, CA:].reshape(NW, ROWS, CB)
            if off:
                send(tb.at[it, to], bz.at[it, off], cbs_sem.at[it, 0], cbr_sem.at[it, 0], zpeer(off))
            for k in WFAR:
                send(
                    ta.at[it, to, lax.rem(w + k, NW)], fromw.at[it, off, k],
                    ts_sem.at[it], tr_sem.at[it, off], wpeer(k),
                )

    def reduce_block(it, off):
        to = lax.rem(z + off, NZ)
        landed(fromw.at[it, off, pl.ds(1, NW - 1)], tr_sem.at[it, off], wpeer(1))
        total = ta[it, to, w].astype(F32)
        for k in range(1, NW):
            total = total + fromw[it, off, k].astype(F32)
        if off:
            toz[it, off] = total.astype(BF)
            send(toz.at[it, off], fromz.at[it, off], us_sem.at[it], ur_sem.at[it], zpeer(off))
        return total

    def reduce_turn(it):
        landed(bz.at[it, pl.ds(1, NZ - 1)], cbr_sem.at[it, 0], zpeer(1))
        total = tb[it, z].astype(F32)
        for k in range(1, NZ):
            total = total + bz[it, k].astype(F32)
        tow[it] = total.astype(BF)
        for k in WFAR:
            send(tow.at[it, lax.rem(w + k, NW)], bw.at[it, k], cbs_sem.at[it, 1], cbr_sem.at[it, 1], wpeer(k))

    def reduce_end(it, total):
        landed(bw.at[it, pl.ds(1, NW - 1)], cbr_sem.at[it, 1], wpeer(1))
        total_b = tow[it, w].astype(F32)
        for k in range(1, NW):
            total_b = total_b + bw[it, k].astype(F32)
        landed(fromz.at[it, pl.ds(1, NZ - 1)], ur_sem.at[it], zpeer(1))
        for k in range(1, NZ):
            total = total + fromz[it, k].astype(F32)
        return jnp.concatenate([total, total_b], axis=1)

    def reduce(it, extra):
        pair = scal_take(2 * it + 1, 0, 3)
        if extra is not None:
            pair = jnp.concatenate([pair[0:1], extra[0:1], pair[2:8]], axis=0)
        scal_send(2 * it + 1, 1, 1, pair)
        terms(it)
        scal_send(2 * it + 1, 2, 2, scal_take(2 * it + 1, 1, 1))
        for off in FAR[:5]:
            reduce_block(it, off)
        reduce_turn(it)
        for off in FAR[5:]:
            total = reduce_block(it, off)
        total = reduce_end(it, total)
        return total, jnp.sum(scal_take(2 * it + 1, 2, 2), axis=1, keepdims=True)

    curve(0, lambda: None)
    ag, sums = reduce(0, scal_take(0, 0, 0))
    energy0, gg = sums[0:1], sums[1:2]
    alpha0 = gg / (energy0 + DAMPING * gg)
    r1 = g - alpha0 * (ag + DAMPING * g)
    gather_start(1, r1.astype(BF))
    scal_send(2, 0, 0, jnp.concatenate([fold(r1 * r1), fold(r1 * g), jnp.zeros((6, 128), F32)], axis=0))
    gather_forward(1, 1)
    gather_forward(1, 7)
    scal_send(2, 1, 1, scal_take(2, 0, 0))
    gather_turn(1)
    gather_forward(1, 2)
    gather_forward(1, 6)
    gather_forward(1, 3)
    gather_forward(1, 5)
    gather_forward(1, 4)
    scal_send(2, 2, 2, scal_take(2, 1, 1))
    gather_end(1)
    norms = []

    def get_beta():
        sums = jnp.sum(scal_take(2, 2, 2), axis=1, keepdims=True)
        norms.extend([sums[0:1], sums[1:2], sums[0:1] / gg])
        return norms[2]

    curve(1, get_beta)
    rr1, rg, beta = norms
    ad1, sums = reduce(1, None)
    energy1 = sums[0:1]
    d1 = r1 + beta * g
    alpha1 = rr1 / (energy1 + DAMPING * (rr1 + 2.0 * beta * rg + beta * beta * gg))
    out[0] = alpha0 * g + alpha1 * d1
    out[1] = r1 - alpha1 * (ad1 + DAMPING * d1)

    for it in range(2):
        sent(va.at[it, 0, pl.ds(0, NZ - 1)], zs_sem.at[it], zpeer(1))
        sent(va.at[it, pl.ds(0, NW - 1)], ws_sem.at[it], wpeer(1))
        sent(vb.at[it, 0, pl.ds(0, NW - 1)], bs_sem.at[it, 0], wpeer(1))
        sent(vb.at[it, pl.ds(0, NZ - 1)], bs_sem.at[it, 1], zpeer(1))
        sent(tb.at[it, pl.ds(0, NZ - 1)], cbs_sem.at[it, 0], zpeer(1))
        sent(tow.at[it, pl.ds(0, NW - 1)], cbs_sem.at[it, 1], wpeer(1))
        sent(give.at[it], cs_sem.at[it], sibling)
        sent(half.at[it], ls_sem.at[it], beside)
        sent(gy.at[it], gs_sem.at[it], sibling)
        sent(ta.at[it, pl.ds(0, NW - 1)], ts_sem.at[it], wpeer(1))
        sent(toz.at[it, pl.ds(1, NZ - 1)], us_sem.at[it], zpeer(1))
    for a in range(4):
        for phase, n in enumerate(((NM,), (2, NW, NZ), (NM, NW, NZ), (2, NW, NZ))[a]):
            sent(sc_in.at[a, phase, pl.ds(1, n - 1)], as_sem.at[a, phase], mpeer(1))
    sent(x.at[share(kept, core)], xs_sem.at[0], across)
    sent(wrow.at[0], xs_sem.at[1], across)
    sent(x.at[share(taken, core)], xs_sem.at[2], sibling)


def on_device(frames, norm_gain, w_inner, w_outer, lengths, frame_mask, gradient):
    hbm = pl.BlockSpec(memory_space=pl.ANY)
    vmem = pl.BlockSpec(memory_space=pltpu.VMEM)
    smem = pl.BlockSpec(memory_space=pltpu.SMEM)
    dma = pltpu.SemaphoreType.DMA
    both = (
        pl.pallas_call(
            kernel,
            out_shape=jax.ShapeDtypeStruct((2, ROWS, F), F32),
            in_specs=[hbm, hbm, hbm, hbm, smem, hbm, hbm],
            out_specs=vmem,
            scratch_shapes=[
                pltpu.VMEM((ROWS, F), F32),
                pltpu.VMEM((1, D), F32),
                pltpu.VMEM((NT, CH), jnp.int32),
                pltpu.VMEM((TOK, D), BF),
                pltpu.VMEM((D, F), BF),
                pltpu.VMEM((2, F, HALF), BF),
                pltpu.VMEM((2, HALF, F), BF),
                pltpu.VMEM((TOK, D), BF),
                pltpu.VMEM((D, TOK), BF),
                pltpu.VMEM((TOK, F), F32),
                pltpu.VMEM((TOK, 128), F32),
                pltpu.VMEM((2, 8, 128), F32),
                pltpu.VMEM((2, NZ, NW, ROWS, CA), BF),
                pltpu.VMEM((2, NZ, NW, ROWS, CB), BF),
                pltpu.VMEM((NT, CH, HALF), F32),
                pltpu.VMEM((NT, CH, HALF), F32),
                pltpu.VMEM((2, NT, CH, HALF), BF),
                pltpu.VMEM((2, NT, CH, HALF), BF),
                pltpu.VMEM((2, NT, CH, HALF), BF),
                pltpu.VMEM((2, NT, CH, HALF), BF),
                pltpu.VMEM((2, NT, CH, HALF), BF),
                pltpu.VMEM((2, NT, CH, HALF), BF),
                pltpu.VMEM((TOK, F), BF),
                pltpu.VMEM((2, NZ, NW, ROWS, CA), BF),
                pltpu.VMEM((2, NZ, NW, ROWS, CB), BF),
                pltpu.VMEM((2, NZ, NW, ROWS, CA), BF),
                pltpu.VMEM((2, NZ, ROWS, CA), BF),
                pltpu.VMEM((2, NZ, ROWS, CA), BF),
                pltpu.VMEM((2, NZ, NW, ROWS, CB), BF),
                pltpu.VMEM((2, NW, ROWS, CB), BF),
                pltpu.VMEM((2, NW, ROWS, CB), BF),
                pltpu.VMEM((4, 3, 8, 128), F32),
                pltpu.VMEM((4, 3, 8, 8, 128), F32),
                dma((8,)),
                dma((2,)), dma((2, NZ)),
                dma((2,)), dma((2,)),
                dma((2,)), dma((2, NT)),
                dma((2,)), dma((2, NT)),
                dma((2,)), dma((2, NT)),
                dma((2,)), dma((2, NZ)),
                dma((2,)), dma((2,)),
                dma((4, 3)), dma((4, 3)),
                dma((3,)), dma((3,)),
                dma((2, 2)), dma((2, 2)),
                dma((2, 2)), dma((2, 2)),
            ],
            compiler_params=pltpu.CompilerParams(
                collective_id=0, has_side_effects=True, vmem_limit_bytes=63 << 20
            ),
            cost_estimate=pl.CostEstimate(flops=9 * 2 * TOK * D * F, bytes_accessed=4 << 20, transcendentals=TOK * F),
        )(
            frames, norm_gain.reshape(1, D), w_inner, w_outer, lengths, frame_mask.reshape(NT, CH), gradient,
        )
    )
    return both[0], both[1]


def solution(mesh):
    return jax.shard_map(
        on_device,
        mesh=mesh,
        in_specs=(
            P("dp", None),
            P(),
            P(None, "mp"),
            P("mp", None),
            P("dp", None),
            P("dp"),
            P("dp", "mp"),
        ),
        out_specs=(P("dp", "mp"), P("dp", "mp")),
        check_vma=False,
    )
```

```python
import jax
import jax.numpy as jnp
from jax import lax
from jax.experimental import pallas as pl
from jax.experimental.pallas import tpu as pltpu
from jax.sharding import PartitionSpec as P

MESH = pl.DeviceIdType.MESH
NZ, NW, NM = 8, 8, 4
ROWS = 16
TOK, D, F, HALF = 512, 1024, 512, 512
CH = 128
SHARE = CH // 2
NT = TOK // CH
BLK = NW * ROWS
CA, CB = 384, 128
DAMPING = 0.03
BF, F32 = jnp.bfloat16, jnp.float32
NEAR = (1, 7, 2, 6, 3, 5, 4)
FAR = (4, 3, 5, 2, 6, 1, 7, 0)
WFAR = (3, 5, 7, 1, 4, 2, 6)
ORDER = (0, 2, 1, 3)


def dot(a, b):
    return jnp.dot(a, b, preferred_element_type=F32)


def fold(p):
    s = jnp.sum(p, axis=0, keepdims=True)
    return s[:, 0:128] + s[:, 128:256] + s[:, 256:384] + s[:, 384:512]


def kernel(
    frames, gain_in, w_inner, w_outer, lengths, mask_in, grad_in, out,
    grad, gain, mask, x, wi, wo, wot, normed, normed_t, hs, wcol,
    wrow, va, vb, u_first, own, give, got, half, theirs, gy, gyo, ga, ta, tb, fromw, toz, fromz, bz, tow, bw, sc_own, sc_in,
    in_sem, zs_sem, zr_sem, ws_sem, wr_sem, cs_sem, cr_sem, ls_sem, lr_sem, gs_sem, gr_sem,
    ts_sem, tr_sem, us_sem, ur_sem, as_sem, ar_sem, xs_sem, xr_sem, bs_sem, br_sem, cbs_sem, cbr_sem,
):
    dp, mp = lax.axis_index("dp"), lax.axis_index("mp")
    z, w = dp // NW, dp % NW
    xl, core = mp // 2, mp % 2
    sibling = (dp, xl * 2 + (1 - core))
    xh = w % 2
    beside = (dp, (1 - xl) * 2 + core)
    across = (dp + 1 - 2 * xh, (1 - xl) * 2 + core)
    kept, taken = 2 + xl, 3 - xl
    kept_from = 2 + (xh + xl) % 2

    def zpeer(k):
        return (lax.rem(z + k, NZ) * NW + w, mp)

    def wpeer(k):
        return (z * NW + lax.rem(w + k, NW), mp)

    def mpeer(k):
        return (dp, lax.rem(mp + k, NM))

    def send(src, dst, ssem, rsem, dev):
        pltpu.make_async_remote_copy(
            src_ref=src, dst_ref=dst, send_sem=ssem, recv_sem=rsem, device_id=dev, device_id_type=MESH
        ).start()

    def landed(ref, rsem, dev):
        pltpu.make_async_remote_copy(
            src_ref=ref, dst_ref=ref, send_sem=rsem, recv_sem=rsem, device_id=dev, device_id_type=MESH
        ).wait_recv()

    def sent(ref, ssem, dev):
        pltpu.make_async_remote_copy(
            src_ref=ref, dst_ref=ref, send_sem=ssem, recv_sem=ssem, device_id=dev, device_id_type=MESH
        ).wait_send()

    barrier = pltpu.get_barrier_semaphore()
    greeted = [zpeer(k) for k in NEAR[::-1]] + [wpeer(k) for k in WFAR] + [mpeer(k) for k in range(1, NM)] + [across]
    for device in greeted:
        pl.semaphore_signal(barrier, inc=1, device_id=device, device_id_type=MESH)

    small = [
        pltpu.make_async_copy(grad_in, grad, in_sem.at[4]),
        pltpu.make_async_copy(gain_in, gain, in_sem.at[5]),
        pltpu.make_async_copy(mask_in, mask, in_sem.at[6]),
    ]
    for c in small:
        c.start()
    def chunk(t):
        return pl.ds(pl.multiple_of(t * CH, CH), CH)

    def share(t, c):
        return pl.ds(pl.multiple_of(t * CH + c * SHARE, SHARE), SHARE)

    loads = [
        pltpu.make_async_copy(frames.at[pl.ds(0, 2 * CH)], x.at[pl.ds(0, 2 * CH)], in_sem.at[0]),
        pltpu.make_async_copy(frames.at[chunk(kept_from)], x.at[chunk(kept)], in_sem.at[7]),
        pltpu.make_async_copy(w_inner, wi, in_sem.at[1]),
        pltpu.make_async_copy(w_outer.at[:, pl.ds(pl.multiple_of(core * HALF, HALF), HALF)], wo.at[0], in_sem.at[2]),
        pltpu.make_async_copy(w_outer.at[:, pl.ds(pl.multiple_of((1 - core) * HALF, HALF), HALF)], wo.at[1], in_sem.at[3]),
    ]
    for c in loads:
        c.start()
    def gather_own(it, rows):
        va[it, z, w] = rows[:, :CA]
        vb[it, z, w] = rows[:, CA:]

    for c in small:
        c.wait()
    g = grad[...]
    gather_own(0, g.astype(BF))
    pl.semaphore_wait(barrier, len(greeted))

    def gather_pass(it, block):
        for k in WFAR:
            send(va.at[it, block, w], va.at[it, block, w], ws_sem.at[it], wr_sem.at[it], wpeer(k))

    def gather_start(it):
        for k in NEAR:
            send(va.at[it, z, w], va.at[it, z, w], zs_sem.at[it], zr_sem.at[it, k], zpeer(k))
        for k in WFAR:
            send(vb.at[it, z, w], vb.at[it, z, w], bs_sem.at[it, 0], br_sem.at[it, 0], wpeer(k))
        gather_pass(it, z)

    def gather_forward(it, k):
        block = lax.rem(z + NZ - k, NZ)
        landed(va.at[it, block, w], zr_sem.at[it, k], zpeer(k))
        gather_pass(it, block)

    def gather_turn(it):
        landed(vb.at[it, 0, pl.ds(0, NW - 1)], br_sem.at[it, 0], wpeer(1))
        for k in NEAR[::-1]:
            send(vb.at[it, z], vb.at[it, z], bs_sem.at[it, 1], br_sem.at[it, 1], zpeer(k))

    def gather_end(it):
        landed(va.at[it, pl.ds(0, NW - 1)], wr_sem.at[it], wpeer(1))
        landed(vb.at[it, pl.ds(0, NZ - 1)], br_sem.at[it, 1], zpeer(1))

    peers_of = (mpeer, wpeer, zpeer, lambda k: sibling)
    count_of = (NM, NW, NZ, 2)

    def scal_send(a, phase, kind, tile):
        sc_own[a, phase] = tile
        for k in range(1, count_of[kind]):
            send(sc_own.at[a, phase], sc_in.at[a, phase, k], as_sem.at[a, phase], ar_sem.at[a, phase], peers_of[kind](k))

    def scal_take(a, phase, kind):
        n = count_of[kind]
        landed(sc_in.at[a, phase, pl.ds(1, n - 1)], ar_sem.at[a, phase], peers_of[kind](1))
        tile = sc_own[a, phase]
        for k in range(1, n):
            tile = tile + sc_in[a, phase, k]
        return tile

    gather_start(0)
    scal_send(0, 0, 0, jnp.broadcast_to(fold(g * g), (8, 128)))

    send(
        frames.at[share(kept_from, core)], x.at[share(kept, core)], xs_sem.at[0], xr_sem.at[0], across
    )

    ends, end = [], jnp.int32(0)
    starts = []
    for j in range(8):
        starts.append(end)
        end = end + lengths[0, j]
        ends.append(end)

    def weight_row(t):
        pos = lax.broadcasted_iota(jnp.int32, (8, 128), 1) + t * CH
        per = jnp.zeros((8, 128), F32)
        for j in range(8):
            inverse = 1.0 / jnp.full((8, 128), lengths[0, j], jnp.int32).astype(F32)
            per = per + jnp.where((pos >= starts[j]) & (pos < ends[j]), inverse, 0.0)
        return mask[pl.ds(t, 1), :].astype(F32) * per / 512.0

    def weight_column(row):
        rowi = lax.broadcasted_iota(jnp.int32, (CH, 128), 0)
        coli = lax.broadcasted_iota(jnp.int32, (CH, 128), 1)
        spread = jnp.where(rowi == coli, jnp.broadcast_to(row[0:1], (CH, 128)), 0.0)
        return jnp.broadcast_to(jnp.sum(spread, axis=1, keepdims=True), (CH, 128))

    wrow[0] = weight_row(kept_from)
    send(wrow.at[0], wrow.at[1], xs_sem.at[1], xr_sem.at[1], across)
    for t in range(2):
        wcol[chunk(t), :] = weight_column(weight_row(t))
    wcol[chunk(kept), :] = weight_column(wrow[0])

    def norm_chunk(t):
        rows = chunk(t)
        xf = x[rows, :].astype(F32)
        mean = jnp.mean(xf, axis=1, keepdims=True)
        xc = xf - mean
        var = jnp.mean(xc * xc, axis=1, keepdims=True)
        nf = gain[...] * xc / jnp.sqrt(var + 1e-05)
        normed[rows, :] = nf.astype(BF)
        normed_t[:, rows] = nf.T.astype(BF)

    def slope_chunk(t):
        rows = chunk(t)
        pre = dot(normed[rows, :], wi[...])
        sig = jax.nn.sigmoid(pre)
        hs[rows, :] = 0.5 * (sig * (1.0 + pre * (1.0 - sig)))

    loads[0].wait()
    norm_chunk(0)
    norm_chunk(1)
    gather_forward(0, 1)
    gather_forward(0, 7)
    gather_turn(0)
    loads[1].wait()
    norm_chunk(kept)
    gather_forward(0, 2)
    gather_forward(0, 6)
    loads[2].wait()
    slope_chunk(0)
    gather_forward(0, 3)
    gather_forward(0, 5)
    gather_forward(0, 4)
    landed(x.at[share(taken, core)], xr_sem.at[0], across)
    send(x.at[share(taken, core)], x.at[share(taken, core)], xs_sem.at[2], xr_sem.at[2], sibling)
    slope_chunk(1)
    slope_chunk(kept)
    loads[3].wait()
    loads[4].wait()
    for i in range(2):
        wot[i] = wo[i].astype(F32).T.astype(BF)
    landed(wrow.at[1], xr_sem.at[1], across)
    wcol[chunk(taken), :] = weight_column(wrow[1])
    landed(x.at[share(taken, 1 - core)], xr_sem.at[2], sibling)
    norm_chunk(taken)
    slope_chunk(taken)
    gather_end(0)

    def tangent(it, t):
        rows = chunk(t)
        mat = jnp.concatenate([va[it].reshape(D, CA), vb[it].reshape(D, CB)], axis=1)
        q = dot(normed[rows, :], mat)
        hq = (hs[rows, :] * q).astype(BF)
        give[it, t] = dot(hq, wo[1]).astype(BF)
        send(give.at[it, t], got.at[it, t], cs_sem.at[it], cr_sem.at[it, t], sibling)
        own[t] = dot(hq, wo[0])

    def pair_sum(it, t):
        landed(got.at[it, t], cr_sem.at[it, t], sibling)
        half[it, t] = (own[t] + got[it, t].astype(F32)).astype(BF)
        send(half.at[it, t], theirs.at[it, t], ls_sem.at[it], lr_sem.at[it, t], across if t > 1 else beside)

    def weigh(it, t, beta):
        landed(theirs.at[it, t], lr_sem.at[it, t], across if t > 1 else beside)
        u = half[it, t].astype(F32) + theirs[it, t].astype(F32)
        if it == 0:
            u_first[t] = u
        else:
            u = u + beta * u_first[t]
        wc = wcol[chunk(t), :]
        wu = jnp.concatenate([wc] * 4, axis=1) * u
        gy[it, t] = wu.astype(BF)
        send(gy.at[it, t], gyo.at[it, t], gs_sem.at[it], gr_sem.at[it, t], sibling)
        return fold(wu * u)

    def pull_back(it, t):
        landed(gyo.at[it, t], gr_sem.at[it, t], sibling)
        rows = chunk(t)
        gh = dot(gy[it, t], wot[0]) + dot(gyo[it, t], wot[1])
        ga[rows, :] = (hs[rows, :] * gh).astype(BF)

    def curve(it, get_beta):
        tangent(it, ORDER[0])
        for i in range(1, NT):
            tangent(it, ORDER[i])
            pair_sum(it, ORDER[i - 1])
        pair_sum(it, ORDER[NT - 1])
        beta = get_beta()
        energy = weigh(it, ORDER[0], beta)
        for i in range(1, NT):
            energy = energy + weigh(it, ORDER[i], beta)
            pull_back(it, ORDER[i - 1])
        scal_send(2 * it + 1, 0, 3, jnp.broadcast_to(energy, (8, 128)))
        pull_back(it, ORDER[NT - 1])

    def terms(it):
        for off in FAR:
            to = lax.rem(z + off, NZ)
            block = dot(normed_t[pl.ds(pl.multiple_of(to * BLK, BLK), BLK), :], ga[...]).astype(BF)
            ta[it, to] = block[:, :CA].reshape(NW, ROWS, CA)
            tb[it, to] = block[:, CA:].reshape(NW, ROWS, CB)
            if off:
                send(tb.at[it, to], bz.at[it, off], cbs_sem.at[it, 0], cbr_sem.at[it, 0], zpeer(off))
            for k in WFAR:
                send(
                    ta.at[it, to, lax.rem(w + k, NW)], fromw.at[it, off, k],
                    ts_sem.at[it], tr_sem.at[it, off], wpeer(k),
                )

    def reduce_block(it, off):
        to = lax.rem(z + off, NZ)
        landed(fromw.at[it, off, pl.ds(1, NW - 1)], tr_sem.at[it, off], wpeer(1))
        total = ta[it, to, w].astype(F32)
        for k in range(1, NW):
            total = total + fromw[it, off, k].astype(F32)
        if off:
            toz[it, off] = total.astype(BF)
            send(toz.at[it, off], fromz.at[it, off], us_sem.at[it], ur_sem.at[it], zpeer(off))
        return total

    def reduce_turn(it):
        landed(bz.at[it, pl.ds(1, NZ - 1)], cbr_sem.at[it, 0], zpeer(1))
        total = tb[it, z].astype(F32)
        for k in range(1, NZ):
            total = total + bz[it, k].astype(F32)
        tow[it] = total.astype(BF)
        for k in WFAR:
            send(tow.at[it, lax.rem(w + k, NW)], bw.at[it, k], cbs_sem.at[it, 1], cbr_sem.at[it, 1], wpeer(k))

    def reduce_end(it, total):
        landed(bw.at[it, pl.ds(1, NW - 1)], cbr_sem.at[it, 1], wpeer(1))
        total_b = tow[it, w].astype(F32)
        for k in range(1, NW):
            total_b = total_b + bw[it, k].astype(F32)
        landed(fromz.at[it, pl.ds(1, NZ - 1)], ur_sem.at[it], zpeer(1))
        for k in range(1, NZ):
            total = total + fromz[it, k].astype(F32)
        return jnp.concatenate([total, total_b], axis=1)

    def reduce(it, extra):
        pair = scal_take(2 * it + 1, 0, 3)
        if extra is not None:
            pair = jnp.concatenate([pair[0:1], extra[0:1], pair[2:8]], axis=0)
        scal_send(2 * it + 1, 1, 1, pair)
        terms(it)
        scal_send(2 * it + 1, 2, 2, scal_take(2 * it + 1, 1, 1))
        for off in FAR[:5]:
            reduce_block(it, off)
        reduce_turn(it)
        for off in FAR[5:]:
            total = reduce_block(it, off)
        total = reduce_end(it, total)
        return total, jnp.sum(scal_take(2 * it + 1, 2, 2), axis=1, keepdims=True)

    curve(0, lambda: None)
    ag, sums = reduce(0, scal_take(0, 0, 0))
    energy0, gg = sums[0:1], sums[1:2]
    alpha0 = gg / (energy0 + DAMPING * gg)
    r1 = g - alpha0 * (ag + DAMPING * g)
    gather_own(1, r1.astype(BF))
    gather_start(1)
    scal_send(2, 0, 0, jnp.concatenate([fold(r1 * r1), fold(r1 * g), jnp.zeros((6, 128), F32)], axis=0))
    gather_forward(1, 1)
    gather_forward(1, 7)
    scal_send(2, 1, 1, scal_take(2, 0, 0))
    gather_turn(1)
    gather_forward(1, 2)
    gather_forward(1, 6)
    gather_forward(1, 3)
    gather_forward(1, 5)
    gather_forward(1, 4)
    scal_send(2, 2, 2, scal_take(2, 1, 1))
    gather_end(1)
    norms = []

    def get_beta():
        sums = jnp.sum(scal_take(2, 2, 2), axis=1, keepdims=True)
        norms.extend([sums[0:1], sums[1:2], sums[0:1] / gg])
        return norms[2]

    curve(1, get_beta)
    rr1, rg, beta = norms
    ad1, sums = reduce(1, None)
    energy1 = sums[0:1]
    d1 = r1 + beta * g
    alpha1 = rr1 / (energy1 + DAMPING * (rr1 + 2.0 * beta * rg + beta * beta * gg))
    out[0] = alpha0 * g + alpha1 * d1
    out[1] = r1 - alpha1 * (ad1 + DAMPING * d1)

    for it in range(2):
        sent(va.at[it, 0, pl.ds(0, NZ - 1)], zs_sem.at[it], zpeer(1))
        sent(va.at[it, pl.ds(0, NW - 1)], ws_sem.at[it], wpeer(1))
        sent(vb.at[it, 0, pl.ds(0, NW - 1)], bs_sem.at[it, 0], wpeer(1))
        sent(vb.at[it, pl.ds(0, NZ - 1)], bs_sem.at[it, 1], zpeer(1))
        sent(tb.at[it, pl.ds(0, NZ - 1)], cbs_sem.at[it, 0], zpeer(1))
        sent(tow.at[it, pl.ds(0, NW - 1)], cbs_sem.at[it, 1], wpeer(1))
        sent(give.at[it], cs_sem.at[it], sibling)
        sent(half.at[it], ls_sem.at[it], beside)
        sent(gy.at[it], gs_sem.at[it], sibling)
        sent(ta.at[it, pl.ds(0, NW - 1)], ts_sem.at[it], wpeer(1))
        sent(toz.at[it, pl.ds(1, NZ - 1)], us_sem.at[it], zpeer(1))
    for a in range(4):
        for phase, n in enumerate(((NM,), (2, NW, NZ), (NM, NW, NZ), (2, NW, NZ))[a]):
            sent(sc_in.at[a, phase, pl.ds(1, n - 1)], as_sem.at[a, phase], mpeer(1))
    sent(x.at[share(kept, core)], xs_sem.at[0], across)
    sent(wrow.at[0], xs_sem.at[1], across)
    sent(x.at[share(taken, core)], xs_sem.at[2], sibling)


def on_device(frames, norm_gain, w_inner, w_outer, lengths, frame_mask, gradient):
    hbm = pl.BlockSpec(memory_space=pl.ANY)
    vmem = pl.BlockSpec(memory_space=pltpu.VMEM)
    smem = pl.BlockSpec(memory_space=pltpu.SMEM)
    dma = pltpu.SemaphoreType.DMA
    both = (
        pl.pallas_call(
            kernel,
            out_shape=jax.ShapeDtypeStruct((2, ROWS, F), F32),
            in_specs=[hbm, hbm, hbm, hbm, smem, hbm, hbm],
            out_specs=vmem,
            scratch_shapes=[
                pltpu.VMEM((ROWS, F), F32),
                pltpu.VMEM((1, D), F32),
                pltpu.VMEM((NT, CH), jnp.int32),
                pltpu.VMEM((TOK, D), BF),
                pltpu.VMEM((D, F), BF),
                pltpu.VMEM((2, F, HALF), BF),
                pltpu.VMEM((2, HALF, F), BF),
                pltpu.VMEM((TOK, D), BF),
                pltpu.VMEM((D, TOK), BF),
                pltpu.VMEM((TOK, F), F32),
                pltpu.VMEM((TOK, 128), F32),
                pltpu.VMEM((2, 8, 128), F32),
                pltpu.VMEM((2, NZ, NW, ROWS, CA), BF),
                pltpu.VMEM((2, NZ, NW, ROWS, CB), BF),
                pltpu.VMEM((NT, CH, HALF), F32),
                pltpu.VMEM((NT, CH, HALF), F32),
                pltpu.VMEM((2, NT, CH, HALF), BF),
                pltpu.VMEM((2, NT, CH, HALF), BF),
                pltpu.VMEM((2, NT, CH, HALF), BF),
                pltpu.VMEM((2, NT, CH, HALF), BF),
                pltpu.VMEM((2, NT, CH, HALF), BF),
                pltpu.VMEM((2, NT, CH, HALF), BF),
                pltpu.VMEM((TOK, F), BF),
                pltpu.VMEM((2, NZ, NW, ROWS, CA), BF),
                pltpu.VMEM((2, NZ, NW, ROWS, CB), BF),
                pltpu.VMEM((2, NZ, NW, ROWS, CA), BF),
                pltpu.VMEM((2, NZ, ROWS, CA), BF),
                pltpu.VMEM((2, NZ, ROWS, CA), BF),
                pltpu.VMEM((2, NZ, NW, ROWS, CB), BF),
                pltpu.VMEM((2, NW, ROWS, CB), BF),
                pltpu.VMEM((2, NW, ROWS, CB), BF),
                pltpu.VMEM((4, 3, 8, 128), F32),
                pltpu.VMEM((4, 3, 8, 8, 128), F32),
                dma((8,)),
                dma((2,)), dma((2, NZ)),
                dma((2,)), dma((2,)),
                dma((2,)), dma((2, NT)),
                dma((2,)), dma((2, NT)),
                dma((2,)), dma((2, NT)),
                dma((2,)), dma((2, NZ)),
                dma((2,)), dma((2,)),
                dma((4, 3)), dma((4, 3)),
                dma((3,)), dma((3,)),
                dma((2, 2)), dma((2, 2)),
                dma((2, 2)), dma((2, 2)),
            ],
            compiler_params=pltpu.CompilerParams(
                collective_id=0, has_side_effects=True, vmem_limit_bytes=63 << 20
            ),
            cost_estimate=pl.CostEstimate(flops=9 * 2 * TOK * D * F, bytes_accessed=4 << 20, transcendentals=TOK * F),
        )(
            frames, norm_gain.reshape(1, D), w_inner, w_outer, lengths, frame_mask.reshape(NT, CH), gradient,
        )
    )
    return both[0], both[1]


def solution(mesh):
    return jax.shard_map(
        on_device,
        mesh=mesh,
        in_specs=(
            P("dp", None),
            P(),
            P(None, "mp"),
            P("mp", None),
            P("dp", None),
            P("dp"),
            P("dp", "mp"),
        ),
        out_specs=(P("dp", "mp"), P("dp", "mp")),
        check_vma=False,
    )
```

```python
import jax
import jax.numpy as jnp
from jax import lax
from jax.experimental import pallas as pl
from jax.experimental.pallas import tpu as pltpu
from jax.sharding import PartitionSpec as P

MESH = pl.DeviceIdType.MESH
NZ, NW, NM = 8, 8, 4
ROWS = 16
TOK, D, F, HALF = 512, 1024, 512, 512
CH = 128
SHARE = CH // 2
NT = TOK // CH
BLK = NW * ROWS
CA, CB = 384, 128
DAMPING = 0.03
BF, F32 = jnp.bfloat16, jnp.float32
NEAR = (1, 7, 2, 6, 3, 5, 4)
FAR = (4, 3, 5, 2, 6, 1, 7, 0)
WFAR = (3, 5, 7, 1, 4, 2, 6)
ORDER = (0, 2, 1, 3)


def dot(a, b):
    return jnp.dot(a, b, preferred_element_type=F32)


def fold(p):
    s = jnp.sum(p, axis=0, keepdims=True)
    return s[:, 0:128] + s[:, 128:256] + s[:, 256:384] + s[:, 384:512]


def kernel(
    frames, gain_in, w_inner, w_outer, lengths, mask_in, grad_in, out,
    grad, gain, mask, x, wi, wo, wot, normed, normed_t, hs, wcol,
    wrow, va, vb, u_first, own, give, got, half, theirs, gy, gyo, ga, ta, tb, fromw, toz, fromz, bz, tow, bw, sc_own, sc_in,
    in_sem, zs_sem, zr_sem, ws_sem, wr_sem, cs_sem, cr_sem, ls_sem, lr_sem, gs_sem, gr_sem,
    ts_sem, tr_sem, us_sem, ur_sem, as_sem, ar_sem, xs_sem, xr_sem, bs_sem, br_sem, cbs_sem, cbr_sem,
):
    dp, mp = lax.axis_index("dp"), lax.axis_index("mp")
    z, w = dp // NW, dp % NW
    xl, core = mp // 2, mp % 2
    sibling = (dp, xl * 2 + (1 - core))
    xh = w % 2
    beside = (dp, (1 - xl) * 2 + core)
    across = (dp + 1 - 2 * xh, (1 - xl) * 2 + core)
    kept, taken = 2 + xl, 3 - xl
    kept_from = 2 + (xh + xl) % 2

    def zpeer(k):
        return (lax.rem(z + k, NZ) * NW + w, mp)

    def wpeer(k):
        return (z * NW + lax.rem(w + k, NW), mp)

    def mpeer(k):
        return (dp, lax.rem(mp + k, NM))

    def send(src, dst, ssem, rsem, dev):
        pltpu.make_async_remote_copy(
            src_ref=src, dst_ref=dst, send_sem=ssem, recv_sem=rsem, device_id=dev, device_id_type=MESH
        ).start()

    def landed(ref, rsem, dev):
        pltpu.make_async_remote_copy(
            src_ref=ref, dst_ref=ref, send_sem=rsem, recv_sem=rsem, device_id=dev, device_id_type=MESH
        ).wait_recv()

    def sent(ref, ssem, dev):
        pltpu.make_async_remote_copy(
            src_ref=ref, dst_ref=ref, send_sem=ssem, recv_sem=ssem, device_id=dev, device_id_type=MESH
        ).wait_send()

    small = [
        pltpu.make_async_copy(grad_in, grad, in_sem.at[4]),
        pltpu.make_async_copy(gain_in, gain, in_sem.at[5]),
        pltpu.make_async_copy(mask_in, mask, in_sem.at[6]),
    ]
    for c in small:
        c.start()
    def chunk(t):
        return pl.ds(pl.multiple_of(t * CH, CH), CH)

    def share(t, c):
        return pl.ds(pl.multiple_of(t * CH + c * SHARE, SHARE), SHARE)

    loads = [
        pltpu.make_async_copy(frames.at[pl.ds(0, 2 * CH)], x.at[pl.ds(0, 2 * CH)], in_sem.at[0]),
        pltpu.make_async_copy(frames.at[chunk(kept_from)], x.at[chunk(kept)], in_sem.at[7]),
        pltpu.make_async_copy(w_inner, wi, in_sem.at[1]),
        pltpu.make_async_copy(w_outer.at[:, pl.ds(pl.multiple_of(core * HALF, HALF), HALF)], wo.at[0], in_sem.at[2]),
        pltpu.make_async_copy(w_outer.at[:, pl.ds(pl.multiple_of((1 - core) * HALF, HALF), HALF)], wo.at[1], in_sem.at[3]),
    ]
    for c in loads:
        c.start()
    barrier = pltpu.get_barrier_semaphore()
    for k in range(1, NZ):
        pl.semaphore_signal(barrier, inc=1, device_id=zpeer(k), device_id_type=MESH)
    for k in range(1, NW):
        pl.semaphore_signal(barrier, inc=1, device_id=wpeer(k), device_id_type=MESH)
    for k in range(1, NM):
        pl.semaphore_signal(barrier, inc=1, device_id=mpeer(k), device_id_type=MESH)
    pl.semaphore_signal(barrier, inc=1, device_id=across, device_id_type=MESH)
    for c in small:
        c.wait()
    pl.semaphore_wait(barrier, NZ + NW + NM - 2)

    def gather_pass(it, block):
        for k in WFAR:
            send(va.at[it, block, w], va.at[it, block, w], ws_sem.at[it], wr_sem.at[it], wpeer(k))

    def gather_start(it, rows):
        va[it, z, w] = rows[:, :CA]
        vb[it, z, w] = rows[:, CA:]
        for k in NEAR:
            send(va.at[it, z, w], va.at[it, z, w], zs_sem.at[it], zr_sem.at[it, k], zpeer(k))
        for k in WFAR:
            send(vb.at[it, z, w], vb.at[it, z, w], bs_sem.at[it, 0], br_sem.at[it, 0], wpeer(k))
        gather_pass(it, z)

    def gather_forward(it, k):
        block = lax.rem(z + NZ - k, NZ)
        landed(va.at[it, block, w], zr_sem.at[it, k], zpeer(k))
        gather_pass(it, block)

    def gather_turn(it):
        landed(vb.at[it, 0, pl.ds(0, NW - 1)], br_sem.at[it, 0], wpeer(1))
        for k in NEAR[::-1]:
            send(vb.at[it, z], vb.at[it, z], bs_sem.at[it, 1], br_sem.at[it, 1], zpeer(k))

    def gather_end(it):
        landed(va.at[it, pl.ds(0, NW - 1)], wr_sem.at[it], wpeer(1))
        landed(vb.at[it, pl.ds(0, NZ - 1)], br_sem.at[it, 1], zpeer(1))

    peers_of = (mpeer, wpeer, zpeer, lambda k: sibling)
    count_of = (NM, NW, NZ, 2)

    def scal_send(a, phase, kind, tile):
        sc_own[a, phase] = tile
        for k in range(1, count_of[kind]):
            send(sc_own.at[a, phase], sc_in.at[a, phase, k], as_sem.at[a, phase], ar_sem.at[a, phase], peers_of[kind](k))

    def scal_take(a, phase, kind):
        n = count_of[kind]
        landed(sc_in.at[a, phase, pl.ds(1, n - 1)], ar_sem.at[a, phase], peers_of[kind](1))
        tile = sc_own[a, phase]
        for k in range(1, n):
            tile = tile + sc_in[a, phase, k]
        return tile

    g = grad[...]
    scal_send(0, 0, 0, jnp.broadcast_to(fold(g * g), (8, 128)))
    gather_start(0, g.astype(BF))

    send(
        frames.at[share(kept_from, core)], x.at[share(kept, core)], xs_sem.at[0], xr_sem.at[0], across
    )

    ends, end = [], jnp.int32(0)
    starts = []
    for j in range(8):
        starts.append(end)
        end = end + lengths[0, j]
        ends.append(end)

    def weight_row(t):
        pos = lax.broadcasted_iota(jnp.int32, (8, 128), 1) + t * CH
        per = jnp.zeros((8, 128), F32)
        for j in range(8):
            inverse = 1.0 / jnp.full((8, 128), lengths[0, j], jnp.int32).astype(F32)
            per = per + jnp.where((pos >= starts[j]) & (pos < ends[j]), inverse, 0.0)
        return mask[pl.ds(t, 1), :].astype(F32) * per / 512.0

    def weight_column(row):
        rowi = lax.broadcasted_iota(jnp.int32, (CH, 128), 0)
        coli = lax.broadcasted_iota(jnp.int32, (CH, 128), 1)
        spread = jnp.where(rowi == coli, jnp.broadcast_to(row[0:1], (CH, 128)), 0.0)
        return jnp.broadcast_to(jnp.sum(spread, axis=1, keepdims=True), (CH, 128))

    wrow[0] = weight_row(kept_from)
    send(wrow.at[0], wrow.at[1], xs_sem.at[1], xr_sem.at[1], across)
    for t in range(2):
        wcol[chunk(t), :] = weight_column(weight_row(t))
    wcol[chunk(kept), :] = weight_column(wrow[0])

    def norm_chunk(t):
        rows = chunk(t)
        xf = x[rows, :].astype(F32)
        mean = jnp.mean(xf, axis=1, keepdims=True)
        xc = xf - mean
        var = jnp.mean(xc * xc, axis=1, keepdims=True)
        nf = gain[...] * xc / jnp.sqrt(var + 1e-05)
        normed[rows, :] = nf.astype(BF)
        normed_t[:, rows] = nf.T.astype(BF)

    def slope_chunk(t):
        rows = chunk(t)
        pre = dot(normed[rows, :], wi[...])
        sig = jax.nn.sigmoid(pre)
        hs[rows, :] = 0.5 * (sig * (1.0 + pre * (1.0 - sig)))

    loads[0].wait()
    norm_chunk(0)
    norm_chunk(1)
    gather_forward(0, 1)
    gather_forward(0, 7)
    gather_turn(0)
    loads[1].wait()
    norm_chunk(kept)
    gather_forward(0, 2)
    gather_forward(0, 6)
    loads[2].wait()
    slope_chunk(0)
    gather_forward(0, 3)
    gather_forward(0, 5)
    gather_forward(0, 4)
    landed(x.at[share(taken, core)], xr_sem.at[0], across)
    send(x.at[share(taken, core)], x.at[share(taken, core)], xs_sem.at[2], xr_sem.at[2], sibling)
    slope_chunk(1)
    slope_chunk(kept)
    loads[3].wait()
    loads[4].wait()
    for i in range(2):
        wot[i] = wo[i].astype(F32).T.astype(BF)
    landed(wrow.at[1], xr_sem.at[1], across)
    wcol[chunk(taken), :] = weight_column(wrow[1])
    landed(x.at[share(taken, 1 - core)], xr_sem.at[2], sibling)
    norm_chunk(taken)
    slope_chunk(taken)
    gather_end(0)

    def tangent(it, t):
        rows = chunk(t)
        mat = jnp.concatenate([va[it].reshape(D, CA), vb[it].reshape(D, CB)], axis=1)
        q = dot(normed[rows, :], mat)
        hq = (hs[rows, :] * q).astype(BF)
        give[it, t] = dot(hq, wo[1]).astype(BF)
        send(give.at[it, t], got.at[it, t], cs_sem.at[it], cr_sem.at[it, t], sibling)
        own[t] = dot(hq, wo[0])

    def pair_sum(it, t):
        landed(got.at[it, t], cr_sem.at[it, t], sibling)
        half[it, t] = (own[t] + got[it, t].astype(F32)).astype(BF)
        send(half.at[it, t], theirs.at[it, t], ls_sem.at[it], lr_sem.at[it, t], across if t > 1 else beside)

    def weigh(it, t, beta):
        landed(theirs.at[it, t], lr_sem.at[it, t], across if t > 1 else beside)
        u = half[it, t].astype(F32) + theirs[it, t].astype(F32)
        if it == 0:
            u_first[t] = u
        else:
            u = u + beta * u_first[t]
        wc = wcol[chunk(t), :]
        wu = jnp.concatenate([wc] * 4, axis=1) * u
        gy[it, t] = wu.astype(BF)
        send(gy.at[it, t], gyo.at[it, t], gs_sem.at[it], gr_sem.at[it, t], sibling)
        return fold(wu * u)

    def pull_back(it, t):
        landed(gyo.at[it, t], gr_sem.at[it, t], sibling)
        rows = chunk(t)
        gh = dot(gy[it, t], wot[0]) + dot(gyo[it, t], wot[1])
        ga[rows, :] = (hs[rows, :] * gh).astype(BF)

    def curve(it, get_beta):
        tangent(it, ORDER[0])
        for i in range(1, NT):
            tangent(it, ORDER[i])
            pair_sum(it, ORDER[i - 1])
        pair_sum(it, ORDER[NT - 1])
        beta = get_beta()
        energy = weigh(it, ORDER[0], beta)
        for i in range(1, NT):
            energy = energy + weigh(it, ORDER[i], beta)
            pull_back(it, ORDER[i - 1])
        scal_send(2 * it + 1, 0, 3, jnp.broadcast_to(energy, (8, 128)))
        pull_back(it, ORDER[NT - 1])

    def terms(it):
        for off in FAR:
            to = lax.rem(z + off, NZ)
            block = dot(normed_t[pl.ds(pl.multiple_of(to * BLK, BLK), BLK), :], ga[...]).astype(BF)
            ta[it, to] = block[:, :CA].reshape(NW, ROWS, CA)
            tb[it, to] = block[:, CA:].reshape(NW, ROWS, CB)
            if off:
                send(tb.at[it, to], bz.at[it, off], cbs_sem.at[it, 0], cbr_sem.at[it, 0], zpeer(off))
            for k in WFAR:
                send(
                    ta.at[it, to, lax.rem(w + k, NW)], fromw.at[it, off, k],
                    ts_sem.at[it], tr_sem.at[it, off], wpeer(k),
                )

    def reduce_block(it, off):
        to = lax.rem(z + off, NZ)
        landed(fromw.at[it, off, pl.ds(1, NW - 1)], tr_sem.at[it, off], wpeer(1))
        total = ta[it, to, w].astype(F32)
        for k in range(1, NW):
            total = total + fromw[it, off, k].astype(F32)
        if off:
            toz[it, off] = total.astype(BF)
            send(toz.at[it, off], fromz.at[it, off], us_sem.at[it], ur_sem.at[it], zpeer(off))
        return total

    def reduce_turn(it):
        landed(bz.at[it, pl.ds(1, NZ - 1)], cbr_sem.at[it, 0], zpeer(1))
        total = tb[it, z].astype(F32)
        for k in range(1, NZ):
            total = total + bz[it, k].astype(F32)
        tow[it] = total.astype(BF)
        for k in WFAR:
            send(tow.at[it, lax.rem(w + k, NW)], bw.at[it, k], cbs_sem.at[it, 1], cbr_sem.at[it, 1], wpeer(k))

    def reduce_end(it, total):
        landed(bw.at[it, pl.ds(1, NW - 1)], cbr_sem.at[it, 1], wpeer(1))
        total_b = tow[it, w].astype(F32)
        for k in range(1, NW):
            total_b = total_b + bw[it, k].astype(F32)
        landed(fromz.at[it, pl.ds(1, NZ - 1)], ur_sem.at[it], zpeer(1))
        for k in range(1, NZ):
            total = total + fromz[it, k].astype(F32)
        return jnp.concatenate([total, total_b], axis=1)

    def reduce(it, extra):
        pair = scal_take(2 * it + 1, 0, 3)
        if extra is not None:
            pair = jnp.concatenate([pair[0:1], extra[0:1], pair[2:8]], axis=0)
        scal_send(2 * it + 1, 1, 1, pair)
        terms(it)
        scal_send(2 * it + 1, 2, 2, scal_take(2 * it + 1, 1, 1))
        for off in FAR[:3]:
            reduce_block(it, off)
        reduce_turn(it)
        for off in FAR[3:]:
            total = reduce_block(it, off)
        total = reduce_end(it, total)
        return total, jnp.sum(scal_take(2 * it + 1, 2, 2), axis=1, keepdims=True)

    curve(0, lambda: None)
    ag, sums = reduce(0, scal_take(0, 0, 0))
    energy0, gg = sums[0:1], sums[1:2]
    alpha0 = gg / (energy0 + DAMPING * gg)
    r1 = g - alpha0 * (ag + DAMPING * g)
    gather_start(1, r1.astype(BF))
    scal_send(2, 0, 0, jnp.concatenate([fold(r1 * r1), fold(r1 * g), jnp.zeros((6, 128), F32)], axis=0))
    gather_forward(1, 1)
    gather_forward(1, 7)
    scal_send(2, 1, 1, scal_take(2, 0, 0))
    gather_turn(1)
    gather_forward(1, 2)
    gather_forward(1, 6)
    gather_forward(1, 3)
    gather_forward(1, 5)
    gather_forward(1, 4)
    scal_send(2, 2, 2, scal_take(2, 1, 1))
    gather_end(1)
    norms = []

    def get_beta():
        sums = jnp.sum(scal_take(2, 2, 2), axis=1, keepdims=True)
        norms.extend([sums[0:1], sums[1:2], sums[0:1] / gg])
        return norms[2]

    curve(1, get_beta)
    rr1, rg, beta = norms
    ad1, sums = reduce(1, None)
    energy1 = sums[0:1]
    d1 = r1 + beta * g
    alpha1 = rr1 / (energy1 + DAMPING * (rr1 + 2.0 * beta * rg + beta * beta * gg))
    out[0] = alpha0 * g + alpha1 * d1
    out[1] = r1 - alpha1 * (ad1 + DAMPING * d1)

    for it in range(2):
        sent(va.at[it, 0, pl.ds(0, NZ - 1)], zs_sem.at[it], zpeer(1))
        sent(va.at[it, pl.ds(0, NW - 1)], ws_sem.at[it], wpeer(1))
        sent(vb.at[it, 0, pl.ds(0, NW - 1)], bs_sem.at[it, 0], wpeer(1))
        sent(vb.at[it, pl.ds(0, NZ - 1)], bs_sem.at[it, 1], zpeer(1))
        sent(tb.at[it, pl.ds(0, NZ - 1)], cbs_sem.at[it, 0], zpeer(1))
        sent(tow.at[it, pl.ds(0, NW - 1)], cbs_sem.at[it, 1], wpeer(1))
        sent(give.at[it], cs_sem.at[it], sibling)
        sent(half.at[it], ls_sem.at[it], beside)
        sent(gy.at[it], gs_sem.at[it], sibling)
        sent(ta.at[it, pl.ds(0, NW - 1)], ts_sem.at[it], wpeer(1))
        sent(toz.at[it, pl.ds(1, NZ - 1)], us_sem.at[it], zpeer(1))
    for a in range(4):
        for phase, n in enumerate(((NM,), (2, NW, NZ), (NM, NW, NZ), (2, NW, NZ))[a]):
            sent(sc_in.at[a, phase, pl.ds(1, n - 1)], as_sem.at[a, phase], mpeer(1))
    sent(x.at[share(kept, core)], xs_sem.at[0], across)
    sent(wrow.at[0], xs_sem.at[1], across)
    sent(x.at[share(taken, core)], xs_sem.at[2], sibling)


def on_device(frames, norm_gain, w_inner, w_outer, lengths, frame_mask, gradient):
    hbm = pl.BlockSpec(memory_space=pl.ANY)
    vmem = pl.BlockSpec(memory_space=pltpu.VMEM)
    smem = pl.BlockSpec(memory_space=pltpu.SMEM)
    dma = pltpu.SemaphoreType.DMA
    both = (
        pl.pallas_call(
            kernel,
            out_shape=jax.ShapeDtypeStruct((2, ROWS, F), F32),
            in_specs=[hbm, hbm, hbm, hbm, smem, hbm, hbm],
            out_specs=vmem,
            scratch_shapes=[
                pltpu.VMEM((ROWS, F), F32),
                pltpu.VMEM((1, D), F32),
                pltpu.VMEM((NT, CH), jnp.int32),
                pltpu.VMEM((TOK, D), BF),
                pltpu.VMEM((D, F), BF),
                pltpu.VMEM((2, F, HALF), BF),
                pltpu.VMEM((2, HALF, F), BF),
                pltpu.VMEM((TOK, D), BF),
                pltpu.VMEM((D, TOK), BF),
                pltpu.VMEM((TOK, F), F32),
                pltpu.VMEM((TOK, 128), F32),
                pltpu.VMEM((2, 8, 128), F32),
                pltpu.VMEM((2, NZ, NW, ROWS, CA), BF),
                pltpu.VMEM((2, NZ, NW, ROWS, CB), BF),
                pltpu.VMEM((NT, CH, HALF), F32),
                pltpu.VMEM((NT, CH, HALF), F32),
                pltpu.VMEM((2, NT, CH, HALF), BF),
                pltpu.VMEM((2, NT, CH, HALF), BF),
                pltpu.VMEM((2, NT, CH, HALF), BF),
                pltpu.VMEM((2, NT, CH, HALF), BF),
                pltpu.VMEM((2, NT, CH, HALF), BF),
                pltpu.VMEM((2, NT, CH, HALF), BF),
                pltpu.VMEM((TOK, F), BF),
                pltpu.VMEM((2, NZ, NW, ROWS, CA), BF),
                pltpu.VMEM((2, NZ, NW, ROWS, CB), BF),
                pltpu.VMEM((2, NZ, NW, ROWS, CA), BF),
                pltpu.VMEM((2, NZ, ROWS, CA), BF),
                pltpu.VMEM((2, NZ, ROWS, CA), BF),
                pltpu.VMEM((2, NZ, NW, ROWS, CB), BF),
                pltpu.VMEM((2, NW, ROWS, CB), BF),
                pltpu.VMEM((2, NW, ROWS, CB), BF),
                pltpu.VMEM((4, 3, 8, 128), F32),
                pltpu.VMEM((4, 3, 8, 8, 128), F32),
                dma((8,)),
                dma((2,)), dma((2, NZ)),
                dma((2,)), dma((2,)),
                dma((2,)), dma((2, NT)),
                dma((2,)), dma((2, NT)),
                dma((2,)), dma((2, NT)),
                dma((2,)), dma((2, NZ)),
                dma((2,)), dma((2,)),
                dma((4, 3)), dma((4, 3)),
                dma((3,)), dma((3,)),
                dma((2, 2)), dma((2, 2)),
                dma((2, 2)), dma((2, 2)),
            ],
            compiler_params=pltpu.CompilerParams(
                collective_id=0, has_side_effects=True, vmem_limit_bytes=63 << 20
            ),
            cost_estimate=pl.CostEstimate(flops=9 * 2 * TOK * D * F, bytes_accessed=4 << 20, transcendentals=TOK * F),
        )(
            frames, norm_gain.reshape(1, D), w_inner, w_outer, lengths, frame_mask.reshape(NT, CH), gradient,
        )
    )
    return both[0], both[1]


def solution(mesh):
    return jax.shard_map(
        on_device,
        mesh=mesh,
        in_specs=(
            P("dp", None),
            P(),
            P(None, "mp"),
            P("mp", None),
            P("dp", None),
            P("dp"),
            P("dp", "mp"),
        ),
        out_specs=(P("dp", "mp"), P("dp", "mp")),
        check_vma=False,
    )
```

```python
import jax
import jax.numpy as jnp
from jax import lax
from jax.experimental import pallas as pl
from jax.experimental.pallas import tpu as pltpu
from jax.sharding import PartitionSpec as P

MESH = pl.DeviceIdType.MESH
NZ, NW, NM = 8, 8, 4
ROWS = 16
TOK, D, F, HALF = 512, 1024, 512, 512
CH = 128
SHARE = CH // 2
NT = TOK // CH
BLK = NW * ROWS
CA, CB = 384, 128
DAMPING = 0.03
BF, F32 = jnp.bfloat16, jnp.float32
NEAR = (1, 7, 2, 6, 3, 5, 4)
FAR = (4, 3, 5, 2, 6, 1, 7, 0)
WFAR = (3, 5, 7, 1, 4, 2, 6)
ORDER = (0, 2, 1, 3)


def dot(a, b):
    return jnp.dot(a, b, preferred_element_type=F32)


def fold(p):
    s = jnp.sum(p, axis=0, keepdims=True)
    return s[:, 0:128] + s[:, 128:256] + s[:, 256:384] + s[:, 384:512]


def kernel(
    frames, gain_in, w_inner, w_outer, lengths, mask_in, grad_in, out,
    grad, gain, mask, x, wi, wo, wot, normed, normed_t, hs, wcol,
    wrow, va, vb, hq, u_first, own, give, got, half, theirs, gy, gyo, ga, ta, tb, fromw, toz, fromz, bz, tow, bw, sc_own, sc_in,
    in_sem, zs_sem, zr_sem, ws_sem, wr_sem, cs_sem, cr_sem, ls_sem, lr_sem, gs_sem, gr_sem,
    ts_sem, tr_sem, us_sem, ur_sem, as_sem, ar_sem, xs_sem, xr_sem, bs_sem, br_sem, cbs_sem, cbr_sem,
):
    dp, mp = lax.axis_index("dp"), lax.axis_index("mp")
    z, w = dp // NW, dp % NW
    xl, core = mp // 2, mp % 2
    sibling = (dp, xl * 2 + (1 - core))
    xh = w % 2
    beside = (dp, (1 - xl) * 2 + core)
    across = (dp + 1 - 2 * xh, (1 - xl) * 2 + core)
    kept, taken = 2 + xl, 3 - xl
    kept_from = 2 + (xh + xl) % 2

    def zpeer(k):
        return (lax.rem(z + k, NZ) * NW + w, mp)

    def wpeer(k):
        return (z * NW + lax.rem(w + k, NW), mp)

    def mpeer(k):
        return (dp, lax.rem(mp + k, NM))

    def send(src, dst, ssem, rsem, dev):
        pltpu.make_async_remote_copy(
            src_ref=src, dst_ref=dst, send_sem=ssem, recv_sem=rsem, device_id=dev, device_id_type=MESH
        ).start()

    def landed(ref, rsem, dev):
        pltpu.make_async_remote_copy(
            src_ref=ref, dst_ref=ref, send_sem=rsem, recv_sem=rsem, device_id=dev, device_id_type=MESH
        ).wait_recv()

    def sent(ref, ssem, dev):
        pltpu.make_async_remote_copy(
            src_ref=ref, dst_ref=ref, send_sem=ssem, recv_sem=ssem, device_id=dev, device_id_type=MESH
        ).wait_send()

    small = [
        pltpu.make_async_copy(grad_in, grad, in_sem.at[4]),
        pltpu.make_async_copy(gain_in, gain, in_sem.at[5]),
        pltpu.make_async_copy(mask_in, mask, in_sem.at[6]),
    ]
    for c in small:
        c.start()
    def chunk(t):
        return pl.ds(pl.multiple_of(t * CH, CH), CH)

    def share(t, c):
        return pl.ds(pl.multiple_of(t * CH + c * SHARE, SHARE), SHARE)

    loads = [
        pltpu.make_async_copy(frames.at[pl.ds(0, 2 * CH)], x.at[pl.ds(0, 2 * CH)], in_sem.at[0]),
        pltpu.make_async_copy(frames.at[chunk(kept_from)], x.at[chunk(kept)], in_sem.at[7]),
        pltpu.make_async_copy(w_inner, wi, in_sem.at[1]),
        pltpu.make_async_copy(w_outer.at[:, pl.ds(pl.multiple_of(core * HALF, HALF), HALF)], wo.at[0], in_sem.at[2]),
        pltpu.make_async_copy(w_outer.at[:, pl.ds(pl.multiple_of((1 - core) * HALF, HALF), HALF)], wo.at[1], in_sem.at[3]),
    ]
    for c in loads:
        c.start()
    barrier = pltpu.get_barrier_semaphore()
    for k in range(1, NZ):
        pl.semaphore_signal(barrier, inc=1, device_id=zpeer(k), device_id_type=MESH)
    for k in range(1, NW):
        pl.semaphore_signal(barrier, inc=1, device_id=wpeer(k), device_id_type=MESH)
    for k in range(1, NM):
        pl.semaphore_signal(barrier, inc=1, device_id=mpeer(k), device_id_type=MESH)
    pl.semaphore_signal(barrier, inc=1, device_id=across, device_id_type=MESH)
    for c in small:
        c.wait()
    pl.semaphore_wait(barrier, NZ + NW + NM - 2)

    def gather_pass(it, block):
        for k in WFAR:
            send(va.at[it, block, w], va.at[it, block, w], ws_sem.at[it], wr_sem.at[it], wpeer(k))

    def gather_start(it, rows):
        va[it, z, w] = rows[:, :CA]
        vb[it, z, w] = rows[:, CA:]
        for k in NEAR:
            send(va.at[it, z, w], va.at[it, z, w], zs_sem.at[it], zr_sem.at[it, k], zpeer(k))
        for k in WFAR:
            send(vb.at[it, z, w], vb.at[it, z, w], bs_sem.at[it, 0], br_sem.at[it, 0], wpeer(k))
        gather_pass(it, z)

    def gather_forward(it, k):
        block = lax.rem(z + NZ - k, NZ)
        landed(va.at[it, block, w], zr_sem.at[it, k], zpeer(k))
        gather_pass(it, block)

    def gather_turn(it):
        landed(vb.at[it, 0, pl.ds(0, NW - 1)], br_sem.at[it, 0], wpeer(1))
        for k in NEAR[::-1]:
            send(vb.at[it, z], vb.at[it, z], bs_sem.at[it, 1], br_sem.at[it, 1], zpeer(k))

    def gather_end(it):
        landed(va.at[it, pl.ds(0, NW - 1)], wr_sem.at[it], wpeer(1))
        landed(vb.at[it, pl.ds(0, NZ - 1)], br_sem.at[it, 1], zpeer(1))

    peers_of = (mpeer, wpeer, zpeer, lambda k: sibling)
    count_of = (NM, NW, NZ, 2)

    def scal_send(a, phase, kind, tile):
        sc_own[a, phase] = tile
        for k in range(1, count_of[kind]):
            send(sc_own.at[a, phase], sc_in.at[a, phase, k], as_sem.at[a, phase], ar_sem.at[a, phase], peers_of[kind](k))

    def scal_take(a, phase, kind):
        n = count_of[kind]
        landed(sc_in.at[a, phase, pl.ds(1, n - 1)], ar_sem.at[a, phase], peers_of[kind](1))
        tile = sc_own[a, phase]
        for k in range(1, n):
            tile = tile + sc_in[a, phase, k]
        return tile

    g = grad[...]
    scal_send(0, 0, 0, jnp.broadcast_to(fold(g * g), (8, 128)))
    gather_start(0, g.astype(BF))

    send(
        frames.at[share(kept_from, core)], x.at[share(kept, core)], xs_sem.at[0], xr_sem.at[0], across
    )

    ends, end = [], jnp.int32(0)
    starts = []
    for j in range(8):
        starts.append(end)
        end = end + lengths[0, j]
        ends.append(end)

    def weight_row(t):
        pos = lax.broadcasted_iota(jnp.int32, (8, 128), 1) + t * CH
        per = jnp.zeros((8, 128), F32)
        for j in range(8):
            inverse = 1.0 / jnp.full((8, 128), lengths[0, j], jnp.int32).astype(F32)
            per = per + jnp.where((pos >= starts[j]) & (pos < ends[j]), inverse, 0.0)
        return mask[pl.ds(t, 1), :].astype(F32) * per / 512.0

    def weight_column(row):
        rowi = lax.broadcasted_iota(jnp.int32, (CH, 128), 0)
        coli = lax.broadcasted_iota(jnp.int32, (CH, 128), 1)
        spread = jnp.where(rowi == coli, jnp.broadcast_to(row[0:1], (CH, 128)), 0.0)
        return jnp.broadcast_to(jnp.sum(spread, axis=1, keepdims=True), (CH, 128))

    wrow[0] = weight_row(kept_from)
    send(wrow.at[0], wrow.at[1], xs_sem.at[1], xr_sem.at[1], across)
    for t in range(2):
        wcol[chunk(t), :] = weight_column(weight_row(t))
    wcol[chunk(kept), :] = weight_column(wrow[0])

    def norm_chunk(t):
        rows = chunk(t)
        xf = x[rows, :].astype(F32)
        mean = jnp.mean(xf, axis=1, keepdims=True)
        xc = xf - mean
        var = jnp.mean(xc * xc, axis=1, keepdims=True)
        nf = gain[...] * xc / jnp.sqrt(var + 1e-05)
        normed[rows, :] = nf.astype(BF)
        normed_t[:, rows] = nf.T.astype(BF)

    def slope_chunk(t):
        rows = chunk(t)
        pre = dot(normed[rows, :], wi[...])
        sig = jax.nn.sigmoid(pre)
        hs[rows, :] = 0.5 * (sig * (1.0 + pre * (1.0 - sig)))

    loads[0].wait()
    norm_chunk(0)
    norm_chunk(1)
    gather_forward(0, 1)
    gather_forward(0, 7)
    gather_turn(0)
    loads[1].wait()
    norm_chunk(kept)
    gather_forward(0, 2)
    gather_forward(0, 6)
    loads[2].wait()
    slope_chunk(0)
    gather_forward(0, 3)
    gather_forward(0, 5)
    gather_forward(0, 4)
    landed(x.at[share(taken, core)], xr_sem.at[0], across)
    send(x.at[share(taken, core)], x.at[share(taken, core)], xs_sem.at[2], xr_sem.at[2], sibling)
    slope_chunk(1)
    slope_chunk(kept)
    loads[3].wait()
    loads[4].wait()
    for i in range(2):
        wot[i] = wo[i].astype(F32).T.astype(BF)
    landed(wrow.at[1], xr_sem.at[1], across)
    wcol[chunk(taken), :] = weight_column(wrow[1])
    landed(x.at[share(taken, 1 - core)], xr_sem.at[2], sibling)
    norm_chunk(taken)
    slope_chunk(taken)
    gather_end(0)

    def project(it, rows):
        mat = jnp.concatenate([va[it].reshape(D, CA), vb[it].reshape(D, CB)], axis=1)
        hq[rows, :] = (hs[rows, :] * dot(normed[rows, :], mat)).astype(BF)

    def tangent(it, t):
        rows = chunk(t)
        give[it, t] = dot(hq[rows, :], wo[1]).astype(BF)
        send(give.at[it, t], got.at[it, t], cs_sem.at[it], cr_sem.at[it, t], sibling)
        own[t] = dot(hq[rows, :], wo[0])

    def pair_sum(it, t):
        landed(got.at[it, t], cr_sem.at[it, t], sibling)
        half[it, t] = (own[t] + got[it, t].astype(F32)).astype(BF)
        send(half.at[it, t], theirs.at[it, t], ls_sem.at[it], lr_sem.at[it, t], across if t > 1 else beside)

    def weigh(it, t, beta):
        landed(theirs.at[it, t], lr_sem.at[it, t], across if t > 1 else beside)
        u = half[it, t].astype(F32) + theirs[it, t].astype(F32)
        if it == 0:
            u_first[t] = u
        else:
            u = u + beta * u_first[t]
        wc = wcol[chunk(t), :]
        wu = jnp.concatenate([wc] * 4, axis=1) * u
        gy[it, t] = wu.astype(BF)
        send(gy.at[it, t], gyo.at[it, t], gs_sem.at[it], gr_sem.at[it, t], sibling)
        return fold(wu * u)

    def pull_back(it, t):
        landed(gyo.at[it, t], gr_sem.at[it, t], sibling)
        rows = chunk(t)
        gh = dot(gy[it, t], wot[0]) + dot(gyo[it, t], wot[1])
        ga[rows, :] = (hs[rows, :] * gh).astype(BF)

    def curve(it, get_beta):
        project(it, pl.ds(0, 2 * CH))
        tangent(it, 0)
        project(it, pl.ds(2 * CH, 2 * CH))
        tangent(it, 2)
        pair_sum(it, 0)
        tangent(it, 1)
        pair_sum(it, 2)
        tangent(it, 3)
        pair_sum(it, 1)
        pair_sum(it, ORDER[NT - 1])
        beta = get_beta()
        energy = weigh(it, ORDER[0], beta)
        for i in range(1, NT):
            energy = energy + weigh(it, ORDER[i], beta)
            pull_back(it, ORDER[i - 1])
        scal_send(2 * it + 1, 0, 3, jnp.broadcast_to(energy, (8, 128)))
        pull_back(it, ORDER[NT - 1])

    def terms(it):
        for off in FAR:
            to = lax.rem(z + off, NZ)
            block = dot(normed_t[pl.ds(pl.multiple_of(to * BLK, BLK), BLK), :], ga[...]).astype(BF)
            ta[it, to] = block[:, :CA].reshape(NW, ROWS, CA)
            tb[it, to] = block[:, CA:].reshape(NW, ROWS, CB)
            if off:
                send(tb.at[it, to], bz.at[it, off], cbs_sem.at[it, 0], cbr_sem.at[it, 0], zpeer(off))
            for k in WFAR:
                send(
                    ta.at[it, to, lax.rem(w + k, NW)], fromw.at[it, off, k],
                    ts_sem.at[it], tr_sem.at[it, off], wpeer(k),
                )

    def reduce_block(it, off):
        to = lax.rem(z + off, NZ)
        landed(fromw.at[it, off, pl.ds(1, NW - 1)], tr_sem.at[it, off], wpeer(1))
        total = ta[it, to, w].astype(F32)
        for k in range(1, NW):
            total = total + fromw[it, off, k].astype(F32)
        if off:
            toz[it, off] = total.astype(BF)
            send(toz.at[it, off], fromz.at[it, off], us_sem.at[it], ur_sem.at[it], zpeer(off))
        return total

    def reduce_turn(it):
        landed(bz.at[it, pl.ds(1, NZ - 1)], cbr_sem.at[it, 0], zpeer(1))
        total = tb[it, z].astype(F32)
        for k in range(1, NZ):
            total = total + bz[it, k].astype(F32)
        tow[it] = total.astype(BF)
        for k in WFAR:
            send(tow.at[it, lax.rem(w + k, NW)], bw.at[it, k], cbs_sem.at[it, 1], cbr_sem.at[it, 1], wpeer(k))

    def reduce_end(it, total):
        landed(bw.at[it, pl.ds(1, NW - 1)], cbr_sem.at[it, 1], wpeer(1))
        total_b = tow[it, w].astype(F32)
        for k in range(1, NW):
            total_b = total_b + bw[it, k].astype(F32)
        landed(fromz.at[it, pl.ds(1, NZ - 1)], ur_sem.at[it], zpeer(1))
        for k in range(1, NZ):
            total = total + fromz[it, k].astype(F32)
        return jnp.concatenate([total, total_b], axis=1)

    def reduce(it, extra):
        pair = scal_take(2 * it + 1, 0, 3)
        if extra is not None:
            pair = jnp.concatenate([pair[0:1], extra[0:1], pair[2:8]], axis=0)
        scal_send(2 * it + 1, 1, 1, pair)
        terms(it)
        scal_send(2 * it + 1, 2, 2, scal_take(2 * it + 1, 1, 1))
        for off in FAR[:5]:
            reduce_block(it, off)
        reduce_turn(it)
        for off in FAR[5:]:
            total = reduce_block(it, off)
        total = reduce_end(it, total)
        return total, jnp.sum(scal_take(2 * it + 1, 2, 2), axis=1, keepdims=True)

    curve(0, lambda: None)
    ag, sums = reduce(0, scal_take(0, 0, 0))
    energy0, gg = sums[0:1], sums[1:2]
    alpha0 = gg / (energy0 + DAMPING * gg)
    r1 = g - alpha0 * (ag + DAMPING * g)
    gather_start(1, r1.astype(BF))
    scal_send(2, 0, 0, jnp.concatenate([fold(r1 * r1), fold(r1 * g), jnp.zeros((6, 128), F32)], axis=0))
    gather_forward(1, 1)
    gather_forward(1, 7)
    scal_send(2, 1, 1, scal_take(2, 0, 0))
    gather_turn(1)
    gather_forward(1, 2)
    gather_forward(1, 6)
    gather_forward(1, 3)
    gather_forward(1, 5)
    gather_forward(1, 4)
    scal_send(2, 2, 2, scal_take(2, 1, 1))
    gather_end(1)
    norms = []

    def get_beta():
        sums = jnp.sum(scal_take(2, 2, 2), axis=1, keepdims=True)
        norms.extend([sums[0:1], sums[1:2], sums[0:1] / gg])
        return norms[2]

    curve(1, get_beta)
    rr1, rg, beta = norms
    ad1, sums = reduce(1, None)
    energy1 = sums[0:1]
    d1 = r1 + beta * g
    alpha1 = rr1 / (energy1 + DAMPING * (rr1 + 2.0 * beta * rg + beta * beta * gg))
    out[0] = alpha0 * g + alpha1 * d1
    out[1] = r1 - alpha1 * (ad1 + DAMPING * d1)

    for it in range(2):
        sent(va.at[it, 0, pl.ds(0, NZ - 1)], zs_sem.at[it], zpeer(1))
        sent(va.at[it, pl.ds(0, NW - 1)], ws_sem.at[it], wpeer(1))
        sent(vb.at[it, 0, pl.ds(0, NW - 1)], bs_sem.at[it, 0], wpeer(1))
        sent(vb.at[it, pl.ds(0, NZ - 1)], bs_sem.at[it, 1], zpeer(1))
        sent(tb.at[it, pl.ds(0, NZ - 1)], cbs_sem.at[it, 0], zpeer(1))
        sent(tow.at[it, pl.ds(0, NW - 1)], cbs_sem.at[it, 1], wpeer(1))
        sent(give.at[it], cs_sem.at[it], sibling)
        sent(half.at[it], ls_sem.at[it], beside)
        sent(gy.at[it], gs_sem.at[it], sibling)
        sent(ta.at[it, pl.ds(0, NW - 1)], ts_sem.at[it], wpeer(1))
        sent(toz.at[it, pl.ds(1, NZ - 1)], us_sem.at[it], zpeer(1))
    for a in range(4):
        for phase, n in enumerate(((NM,), (2, NW, NZ), (NM, NW, NZ), (2, NW, NZ))[a]):
            sent(sc_in.at[a, phase, pl.ds(1, n - 1)], as_sem.at[a, phase], mpeer(1))
    sent(x.at[share(kept, core)], xs_sem.at[0], across)
    sent(wrow.at[0], xs_sem.at[1], across)
    sent(x.at[share(taken, core)], xs_sem.at[2], sibling)


def on_device(frames, norm_gain, w_inner, w_outer, lengths, frame_mask, gradient):
    hbm = pl.BlockSpec(memory_space=pl.ANY)
    vmem = pl.BlockSpec(memory_space=pltpu.VMEM)
    smem = pl.BlockSpec(memory_space=pltpu.SMEM)
    dma = pltpu.SemaphoreType.DMA
    both = (
        pl.pallas_call(
            kernel,
            out_shape=jax.ShapeDtypeStruct((2, ROWS, F), F32),
            in_specs=[hbm, hbm, hbm, hbm, smem, hbm, hbm],
            out_specs=vmem,
            scratch_shapes=[
                pltpu.VMEM((ROWS, F), F32),
                pltpu.VMEM((1, D), F32),
                pltpu.VMEM((NT, CH), jnp.int32),
                pltpu.VMEM((TOK, D), BF),
                pltpu.VMEM((D, F), BF),
                pltpu.VMEM((2, F, HALF), BF),
                pltpu.VMEM((2, HALF, F), BF),
                pltpu.VMEM((TOK, D), BF),
                pltpu.VMEM((D, TOK), BF),
                pltpu.VMEM((TOK, F), F32),
                pltpu.VMEM((TOK, 128), F32),
                pltpu.VMEM((2, 8, 128), F32),
                pltpu.VMEM((2, NZ, NW, ROWS, CA), BF),
                pltpu.VMEM((2, NZ, NW, ROWS, CB), BF),
                pltpu.VMEM((TOK, F), BF),
                pltpu.VMEM((NT, CH, HALF), F32),
                pltpu.VMEM((NT, CH, HALF), F32),
                pltpu.VMEM((2, NT, CH, HALF), BF),
                pltpu.VMEM((2, NT, CH, HALF), BF),
                pltpu.VMEM((2, NT, CH, HALF), BF),
                pltpu.VMEM((2, NT, CH, HALF), BF),
                pltpu.VMEM((2, NT, CH, HALF), BF),
                pltpu.VMEM((2, NT, CH, HALF), BF),
                pltpu.VMEM((TOK, F), BF),
                pltpu.VMEM((2, NZ, NW, ROWS, CA), BF),
                pltpu.VMEM((2, NZ, NW, ROWS, CB), BF),
                pltpu.VMEM((2, NZ, NW, ROWS, CA), BF),
                pltpu.VMEM((2, NZ, ROWS, CA), BF),
                pltpu.VMEM((2, NZ, ROWS, CA), BF),
                pltpu.VMEM((2, NZ, NW, ROWS, CB), BF),
                pltpu.VMEM((2, NW, ROWS, CB), BF),
                pltpu.VMEM((2, NW, ROWS, CB), BF),
                pltpu.VMEM((4, 3, 8, 128), F32),
                pltpu.VMEM((4, 3, 8, 8, 128), F32),
                dma((8,)),
                dma((2,)), dma((2, NZ)),
                dma((2,)), dma((2,)),
                dma((2,)), dma((2, NT)),
                dma((2,)), dma((2, NT)),
                dma((2,)), dma((2, NT)),
                dma((2,)), dma((2, NZ)),
                dma((2,)), dma((2,)),
                dma((4, 3)), dma((4, 3)),
                dma((3,)), dma((3,)),
                dma((2, 2)), dma((2, 2)),
                dma((2, 2)), dma((2, 2)),
            ],
            compiler_params=pltpu.CompilerParams(
                collective_id=0, has_side_effects=True, vmem_limit_bytes=63 << 20
            ),
            cost_estimate=pl.CostEstimate(flops=9 * 2 * TOK * D * F, bytes_accessed=4 << 20, transcendentals=TOK * F),
        )(
            frames, norm_gain.reshape(1, D), w_inner, w_outer, lengths, frame_mask.reshape(NT, CH), gradient,
        )
    )
    return both[0], both[1]


def solution(mesh):
    return jax.shard_map(
        on_device,
        mesh=mesh,
        in_specs=(
            P("dp", None),
            P(),
            P(None, "mp"),
            P("mp", None),
            P("dp", None),
            P("dp"),
            P("dp", "mp"),
        ),
        out_specs=(P("dp", "mp"), P("dp", "mp")),
        check_vma=False,
    )
```
